32 devices in a mesh: space: 4 (over z), chaos: 8 (over y, x, core).
Axes of the slice: x: 2, y: 2, z: 4, core: 2. Of those that a mesh axis runs over, the one named last changes fastest.
Arguments:
- velocity: float32 [40, 3, 4, 64, 128], P('chaos', None, 'space')
- base_velocity: float32 [40, 3, 4, 64, 128], P('chaos', None, 'space')
- mode_slot: int32 [35], replicated, may hold values from 0 to 39, as said below
- triples: int32 [4096, 3], replicated, may hold values from 0 to 34, as said below
- triple_coef: bfloat16 [4096], replicated, may hold values from -0.29882812 to 0.29882812
Outputs:
- convection: float32 [40, 3, 4, 64, 128], P('chaos', None, 'space')
- next_velocity: float32 [40, 3, 4, 64, 128], P('chaos', None, 'space')
The draws below stay inside these ranges and needn't reach their ends.
Inputs may be any that keep to these rules, and one draw needn't show every extreme that they name: `mode_slot`: the modes take distinct slots; slots that hold no mode are zero in velocity and base_velocity. `triples`: each triple (i, j, k) of modes is listed at most once.
All inputs are finite; a program needn't handle non-finite values.
Results may differ from the reference program's by a relative error of at most 0.0052.
Values may be sent and summed in bfloat16 or wider, within the bound.
No kernel may reach another device: no remote copies, remote signals or barrier semaphores. Data moves between devices by JAX's collectives and lax.ppermute only.
A program may use at most 192 MiB of HBM per device.

```python
import jax
import jax.numpy as jnp
from jax import lax

MODES = 35
SLOTS = 40
NY = 64
NZ = 128
NNZ = 4096
NX = 4


def slot_table(key):
    base_key = jax.random.fold_in(key, 101)
    scores = jax.random.permutation(jax.random.fold_in(base_key, 1), SLOTS).astype(jnp.int32)
    scores = scores.at[0].set(-2).at[SLOTS - 1].set(-1)
    chosen = jnp.argsort(scores, stable=True)[:MODES]
    order = jax.random.permutation(jax.random.fold_in(base_key, 2), MODES)
    return chosen[order].astype(jnp.int32)


def live_field(key, salt):
    slots = slot_table(key)
    live = jnp.zeros((SLOTS,), jnp.float32).at[slots].set(1.0)
    noise_key = jax.random.fold_in(key, salt)
    shape = (SLOTS, 3, NX, NY, NZ)
    values = jax.random.normal(noise_key, shape, jnp.float32)
    scales = jnp.exp(jax.random.uniform(jax.random.fold_in(noise_key, 3), (SLOTS, 3, 1, 1, 1), jnp.float32, -1.0, 0.5))
    return values * scales * live[:, None, None, None, None]


def draw_velocity(key, part):
    return live_field(key, 201)


def draw_base_velocity(key, part):
    return live_field(key, 202)


def draw_mode_slot(key, part):
    return slot_table(key)


def draw_triples(key, part):
    flat_index = jax.random.permutation(jax.random.fold_in(key, 301), MODES * MODES * MODES)[:NNZ]
    return jnp.stack([flat_index // (MODES * MODES), flat_index // MODES % MODES, flat_index % MODES], axis=1).astype(jnp.int32)


def gaussian(own_key, extent, width, most, kind=jnp.bfloat16):
    return jnp.clip(width * jax.random.normal(own_key, extent, jnp.float32), -most, most).astype(kind)


def setup_inputs(seed: int = 0) -> dict:
    splits = jax.random.split(jax.random.key(seed), 6)
    return {
        "velocity": draw_velocity(jax.random.fold_in(splits[5], 71), 0),
        "base_velocity": draw_base_velocity(jax.random.fold_in(splits[5], 71), 0),
        "mode_slot": draw_mode_slot(jax.random.fold_in(splits[5], 71), 0),
        "triples": draw_triples(jax.random.fold_in(splits[5], 71), 0),
        "triple_coef": gaussian(splits[4], (NNZ,), 0.05, 0.29882812),
    }


SECTION_STEP = 0.5


def slopes(padded):
    interior = padded[:, :, 1:-1]
    along_x = 0.5 * (padded[:, :, 2:] - padded[:, :, :-2])
    along_y = 0.5 * (jnp.roll(interior, -1, 3) - jnp.roll(interior, 1, 3))
    along_z = 0.5 * (jnp.roll(interior, -1, 4) - jnp.roll(interior, 1, 4))
    return jnp.stack([along_x, along_y, along_z], axis=2)


def reference(velocity, base_velocity, mode_slot, triples, triple_coef):
    rounded = velocity.astype(jnp.bfloat16)
    moving = rounded.astype(jnp.float32)
    padded = jnp.concatenate([moving[:, :, -1:], moving, moving[:, :, :1]], axis=2)
    gradients = slopes(padded).astype(jnp.bfloat16)
    slot_i = mode_slot[triples[:, 0]].astype(jnp.int32)
    slot_j = mode_slot[triples[:, 1]].astype(jnp.int32)
    slot_k = mode_slot[triples[:, 2]].astype(jnp.int32)
    coef_values = triple_coef.astype(jnp.float32)

    def add_triple(running, entry):
        out_slot, left_slot, right_slot, weight = entry
        term = jnp.sum(moving[left_slot][None] * gradients[right_slot].astype(jnp.float32), axis=1)
        return running.at[out_slot].add(weight * term), None

    start_sum = jnp.zeros(moving.shape, jnp.float32)
    convection, _ = lax.scan(add_triple, start_sum, (slot_k, slot_i, slot_j, coef_values))
    next_velocity = base_velocity - SECTION_STEP * convection
    return convection, next_velocity
```

```python
import functools

import jax
import jax.numpy as jnp
from jax import lax
from jax.experimental import pallas as pl
from jax.experimental.pallas import tpu as pltpu
from jax.sharding import PartitionSpec as P

SECTION_STEP = 0.5
COMPS = 3
LANES = 128
MODE_PAD = 40
GROUP = 6
VMEM_LIMIT = 48 * 1024 * 1024


def round_up(value, unit):
    return -(-value // unit) * unit


def vmem_spec():
    return pl.BlockSpec(memory_space=pltpu.VMEM)


def params():
    return pltpu.CompilerParams(vmem_limit_bytes=VMEM_LIMIT)


def pack_kernel(chunks, rows, fields, packed, ny, v_ref, out_ref):
    def row_block(y):
        block = v_ref[pl.ds(y, fields, stride=ny), :]
        pad = jnp.zeros((packed - fields, LANES), jnp.float32)
        return jnp.concatenate([block, pad], axis=0).astype(jnp.bfloat16)

    for y in range(ny):
        block = row_block(y)
        chunk, row = divmod(y, rows)
        out_ref[chunk, row + 1] = block
        if row == 0:
            out_ref[(chunk - 1) % chunks, rows + 1] = block
        if row == rows - 1:
            out_ref[(chunk + 1) % chunks, 0] = block


def table_kernel(groups, triples_ref, coef_ref, out_ref):
    count = triples_ref.shape[1]
    mode_i = triples_ref[0:1, :]
    mode_j = triples_ref[1:2, :]
    mode_k = triples_ref[2:3, :]
    group = jnp.zeros_like(mode_j)
    for g in range(1, groups):
        group = group + (mode_j >= g * GROUP).astype(jnp.int32)
    row = group * MODE_PAD + mode_k
    column = (mode_j - group * GROUP) * MODE_PAD + mode_i
    coef = coef_ref[...].astype(jnp.float32)
    total = jnp.zeros((groups * MODE_PAD, 2 * LANES), jnp.float32)
    step = 1024 if count % 1024 == 0 else count
    row_iota = lax.broadcasted_iota(jnp.int32, (groups * MODE_PAD, step), 0)
    column_iota = lax.broadcasted_iota(jnp.int32, (2 * LANES, step), 0)
    for start in range(0, count, step):
        part = slice(start, start + step)
        left = jnp.where(row_iota == row[:, part], coef[:, part], 0.0).astype(jnp.bfloat16)
        right = jnp.where(column_iota == column[:, part], 1.0, 0.0).astype(jnp.bfloat16)
        total = total + lax.dot_general(
            left, right, (((1,), (1,)), ((), ())), preferred_element_type=jnp.float32
        )
    for g in range(groups):
        out_ref[g] = total[g * MODE_PAD : (g + 1) * MODE_PAD].astype(jnp.bfloat16)


def contract_kernel(
    slot_dev, packed, groups, modes, slot_ref, center_ref, low_ref, high_ref, table_ref, out_ref, slope_ref, prod_ref
):
    chunks, rows = center_ref.shape[0], out_ref.shape[1]
    wide = chunks * packed
    column = lax.broadcasted_iota(jnp.int32, (MODE_PAD, wide), 1)
    mode = lax.broadcasted_iota(jnp.int32, (MODE_PAD, wide), 0)
    owner = jnp.zeros_like(column)
    for s in range(1, chunks):
        owner = owner + (column >= s * packed).astype(jnp.int32)
    inner = column - owner * packed
    local = jnp.zeros_like(column)
    for s in range(1, slot_dev):
        local = local + (inner >= s * COMPS).astype(jnp.int32)
    comp = inner - local * COMPS
    slot = jnp.where(inner < slot_dev * COMPS, owner * slot_dev + local, -1)
    wanted = jnp.full_like(column, -2)
    for m in range(modes):
        wanted = jnp.where(mode == m, slot_ref[m], wanted)
    hit = jnp.where(wanted == slot, 1.0, 0.0)
    pick_f32 = jnp.concatenate([jnp.where(comp == d, hit, 0.0) for d in range(COMPS)], axis=0)
    pick = pick_f32.astype(jnp.bfloat16)
    place = pick_f32.T.astype(jnp.bfloat16)

    def one_row(r, carry):
        def raw(ref, index):
            return ref[:, index].reshape(wide, LANES)

        center = raw(center_ref, r + 1)
        center_f32 = center.astype(jnp.float32)
        along_x = 0.5 * (raw(high_ref, r + 1).astype(jnp.float32) - raw(low_ref, r + 1).astype(jnp.float32))
        along_y = 0.5 * (raw(center_ref, r + 2).astype(jnp.float32) - raw(center_ref, r).astype(jnp.float32))
        along_z = 0.5 * (pltpu.roll(center_f32, LANES - 1, 1) - pltpu.roll(center_f32, 1, 1))
        fields = jnp.concatenate(
            [center, along_x.astype(jnp.bfloat16), along_y.astype(jnp.bfloat16), along_z.astype(jnp.bfloat16)], axis=1
        )
        picked = jnp.dot(pick, fields, preferred_element_type=jnp.float32)
        slope_ref[...] = picked[:, LANES:]
        moving = [picked[d * MODE_PAD : (d + 1) * MODE_PAD, :LANES] for d in range(COMPS)]
        for g in range(groups):
            for c in range(COMPS):
                parts = []
                for inner_j in range(GROUP):
                    at = c * MODE_PAD + g * GROUP + inner_j
                    term = moving[0] * slope_ref[at : at + 1, 0:LANES]
                    for d in range(1, COMPS):
                        term = term + moving[d] * slope_ref[at : at + 1, d * LANES : (d + 1) * LANES]
                    parts.append(term)
                parts.append(jnp.zeros((2 * LANES - GROUP * MODE_PAD, LANES), jnp.float32))
                prod_ref[g, :, c * LANES : (c + 1) * LANES] = jnp.concatenate(parts, axis=0).astype(jnp.bfloat16)
        total = jnp.dot(table_ref[0], prod_ref[0], preferred_element_type=jnp.float32)
        for g in range(1, groups):
            total = total + jnp.dot(table_ref[g], prod_ref[g], preferred_element_type=jnp.float32)
        stacked = jnp.concatenate([total[:, c * LANES : (c + 1) * LANES] for c in range(COMPS)], axis=0)
        placed = jnp.dot(place, stacked.astype(jnp.bfloat16), preferred_element_type=jnp.float32)
        out_ref[:, r] = placed.astype(jnp.bfloat16).reshape(chunks, packed, LANES)
        return carry

    lax.fori_loop(0, rows, one_row, 0)


def finish_kernel(fields, packed, ny, got_ref, base_ref, conv_ref, next_ref, flat_ref):
    chunks, rows = got_ref.shape[0], got_ref.shape[1]
    for chunk in range(chunks):
        for row in range(rows):
            at = (chunk * rows + row) * packed
            flat_ref[at : at + packed, :] = got_ref[chunk, row].astype(jnp.float32)
    for f in range(fields):
        value = flat_ref[pl.ds(f, ny, stride=packed), :]
        conv_ref[f] = value
        next_ref[f] = base_ref[f] - SECTION_STEP * value


def on_device(velocity, base_velocity, mode_slot, triples, triple_coef):
    slot_dev, comps, _, ny, nz = velocity.shape
    chunks = lax.axis_size("chaos")
    planes = lax.axis_size("space")
    modes = mode_slot.shape[0]
    fields = slot_dev * comps
    packed = round_up(fields, 16)
    rows = ny // chunks
    groups = -(-modes // GROUP)
    wide = chunks * packed

    sent = pl.pallas_call(
        functools.partial(pack_kernel, chunks, rows, fields, packed, ny),
        out_shape=jax.ShapeDtypeStruct((chunks, rows + 2, packed, nz), jnp.bfloat16),
        in_specs=[vmem_spec()],
        out_specs=vmem_spec(),
        compiler_params=params(),
        name="pack",
    )(velocity.reshape(fields * ny, nz))
    center = lax.all_to_all(sent, "chaos", 0, 0, tiled=True)
    forward = [(i, (i + 1) % planes) for i in range(planes)]
    backward = [(target, source) for source, target in forward]
    low = lax.ppermute(center, "space", forward)
    high = lax.ppermute(center, "space", backward)
    table = pl.pallas_call(
        functools.partial(table_kernel, groups),
        out_shape=jax.ShapeDtypeStruct((groups, MODE_PAD, 2 * LANES), jnp.bfloat16),
        in_specs=[vmem_spec(), vmem_spec()],
        out_specs=vmem_spec(),
        compiler_params=params(),
        name="table",
    )(triples.T, triple_coef.reshape(1, -1))
    returned = pl.pallas_call(
        functools.partial(contract_kernel, slot_dev, packed, groups, modes),
        out_shape=jax.ShapeDtypeStruct((chunks, rows, packed, nz), jnp.bfloat16),
        in_specs=[pl.BlockSpec(memory_space=pltpu.SMEM)] + [vmem_spec()] * 4,
        out_specs=vmem_spec(),
        scratch_shapes=[
            pltpu.VMEM((COMPS * MODE_PAD, COMPS * LANES), jnp.float32),
            pltpu.VMEM((groups, 2 * LANES, COMPS * LANES), jnp.bfloat16),
        ],
        compiler_params=params(),
        name="contract",
    )(mode_slot, center, low, high, table)
    got = lax.all_to_all(returned, "chaos", 0, 0, tiled=True)
    convection, next_velocity = pl.pallas_call(
        functools.partial(finish_kernel, fields, packed, ny),
        out_shape=[jax.ShapeDtypeStruct((fields, ny, nz), jnp.float32)] * 2,
        in_specs=[vmem_spec(), vmem_spec()],
        out_specs=[vmem_spec(), vmem_spec()],
        scratch_shapes=[pltpu.VMEM((ny * packed, LANES), jnp.float32)],
        compiler_params=params(),
        name="finish",
    )(got, base_velocity.reshape(fields, ny, nz))
    return convection.reshape(velocity.shape), next_velocity.reshape(velocity.shape)


def solution(mesh):
    spread = P("chaos", None, "space", None, None)
    return jax.shard_map(
        on_device,
        mesh=mesh,
        in_specs=(spread, spread, P(), P(), P()),
        out_specs=(spread, spread),
        check_vma=False,
    )
```

```python
import functools

import jax
import jax.numpy as jnp
import numpy as np
from jax import lax
from jax.experimental import pallas as pl
from jax.experimental.pallas import tpu as pltpu
from jax.sharding import PartitionSpec as P

SECTION_STEP = 0.5
COMPS = 3
LANES = 128
TILE = 256
VMEM_LIMIT = 48 * 1024 * 1024


def round_up(value, unit):
    return -(-value // unit) * unit


def vmem_spec():
    return pl.BlockSpec(memory_space=pltpu.VMEM)


def params():
    return pltpu.CompilerParams(vmem_limit_bytes=VMEM_LIMIT)


class Plan:
    def __init__(self, slot_dev, ny, nz, planes, chunks, modes):
        self.slot_dev, self.ny, self.planes, self.chunks, self.modes = slot_dev, ny, planes, chunks, modes
        self.fields = slot_dev * COMPS
        self.packed = round_up(self.fields, 16)
        self.wide = chunks * self.packed
        self.rows = ny // chunks
        self.width = nz // planes
        assert nz == LANES and self.width * planes == nz and self.rows * chunks == ny
        assert planes & (planes - 1) == 0 and 2 * self.rows <= self.width
        self.inner = -(-self.rows // planes)
        if self.rows % planes == 0:
            assert planes >= 3
            self.vectors = self.inner + 1
            first = self.inner * planes
            self.low, self.high, self.side = first, first + 1, first + 2
        else:
            assert self.rows + 3 <= planes
            self.vectors = 1
            self.low, self.high, self.side = planes - 1, self.rows, self.rows + 1
        self.mode_pad = round_up(modes, 8)
        self.main = modes // 16 * 16
        self.rest = modes - self.main
        self.rest_rows = round_up(self.rest * self.mode_pad, 16)
        self.pairs = modes * self.main
        self.depth = round_up(self.pairs + self.rest_rows, TILE)
        self.groups = self.depth // TILE

    def stencil(self):
        out = np.zeros((self.vectors * LANES, 2 * self.inner * LANES), np.float32)
        width = self.width
        for r in range(self.rows):
            above = r + 1 if r + 1 < self.rows else self.high
            below = r - 1 if r > 0 else self.low
            for w in range(width):
                at = r * width + w
                out[above * width + w, at] += 0.5
                out[below * width + w, at] -= 0.5
                right = at + 1 if w + 1 < width else self.side * width + 2 * r + 1
                left = at - 1 if w > 0 else self.side * width + 2 * r
                out[right, self.inner * LANES + at] += 0.5
                out[left, self.inner * LANES + at] -= 0.5
        return out


def swap_blocks(items, width):
    items = list(items)
    count = len(items)
    block = lax.broadcasted_iota(jnp.int32, items[0].shape, 1) // width
    half = count // 2
    while half:
        upper = (block & half) != 0
        for a in range(count):
            if a & half:
                continue
            first, second = items[a], items[a + half]
            items[a] = jnp.where(upper, pltpu.roll(second, half * width, 1), first)
            items[a + half] = jnp.where(upper, second, pltpu.roll(first, LANES - half * width, 1))
        half //= 2
    return items


def pack_kernel(plan, v_ref, out_ref):
    planes, rows, ny, width = plan.planes, plan.rows, plan.ny, plan.width
    zeros = jnp.zeros((plan.packed, LANES), jnp.float32)
    column = lax.broadcasted_iota(jnp.int32, (plan.packed, LANES), 1) % width

    def line(y):
        block = v_ref[pl.ds(y % ny, plan.fields, stride=ny), :]
        if plan.packed == plan.fields:
            return block
        return jnp.concatenate([block, zeros[plan.fields :]], axis=0)

    for chunk in range(plan.chunks):
        first = chunk * rows
        blocks = [zeros] * (plan.vectors * planes)
        side = zeros
        for r in range(rows):
            block = line(first + r)
            blocks[r] = block
            side = jnp.where(column == 2 * r, pltpu.roll(block, 2 * r + 1, 1), side)
            side = jnp.where(column == 2 * r + 1, pltpu.roll(block, (2 * r + 1 - width) % LANES, 1), side)
        blocks[plan.low] = line(first - 1)
        blocks[plan.high] = line(first + rows)
        blocks[plan.side] = side
        for vector in range(plan.vectors):
            swapped = swap_blocks(blocks[vector * planes : (vector + 1) * planes], width)
            for s in range(planes):
                out_ref[s, chunk, vector] = swapped[s].astype(jnp.bfloat16)


def table_kernel(plan, triples_ref, coef_ref, out_ref):
    count = triples_ref.shape[1]
    mode_i = triples_ref[0:1, :]
    mode_j = triples_ref[1:2, :]
    mode_k = triples_ref[2:3, :]
    place = jnp.where(
        mode_i < plan.main,
        mode_j * plan.main + mode_i,
        plan.pairs + (mode_i - plan.main) * plan.mode_pad + mode_j,
    )
    row = (place // TILE) * plan.mode_pad + mode_k
    column = place % TILE
    coef = coef_ref[...].astype(jnp.float32)
    height = plan.groups * plan.mode_pad
    total = jnp.zeros((height, TILE), jnp.float32)
    step = 1024 if count % 1024 == 0 else count
    row_iota = lax.broadcasted_iota(jnp.int32, (height, step), 0)
    column_iota = lax.broadcasted_iota(jnp.int32, (TILE, step), 0)
    for start in range(0, count, step):
        part = slice(start, start + step)
        left = jnp.where(row_iota == row[:, part], coef[:, part], 0.0).astype(jnp.bfloat16)
        right = jnp.where(column_iota == column[:, part], 1.0, 0.0).astype(jnp.bfloat16)
        total = total + lax.dot_general(
            left, right, (((1,), (1,)), ((), ())), preferred_element_type=jnp.float32
        )
    for g in range(plan.groups):
        out_ref[g] = total[g * plan.mode_pad : (g + 1) * plan.mode_pad].astype(jnp.bfloat16)


def mode_picker(plan, slot_ref):
    shape = (plan.mode_pad, plan.wide)
    column = lax.broadcasted_iota(jnp.int32, shape, 1)
    mode = lax.broadcasted_iota(jnp.int32, shape, 0)
    inner = column % plan.packed
    slot = jnp.where(
        inner < plan.fields, (column // plan.packed) * plan.slot_dev + inner // COMPS, -1
    )
    wanted = jnp.full(shape, -2, jnp.int32)
    for m in range(plan.modes):
        wanted = jnp.where(mode == m, slot_ref[m], wanted)
    hit = jnp.where(wanted == slot, 1.0, 0.0)
    return jnp.concatenate([jnp.where(inner % COMPS == d, hit, 0.0) for d in range(COMPS)], axis=0)


def contract_kernel(plan, slot_ref, got_ref, stencil_ref, table_ref, out_ref, field_ref, prod_ref):
    planes, inner, pad = plan.planes, plan.inner, plan.mode_pad
    picker = mode_picker(plan, slot_ref)
    pick = picker.astype(jnp.bfloat16)
    place = picker.T.astype(jnp.bfloat16)
    tail = plan.pairs + plan.rest_rows
    if tail < plan.depth:
        prod_ref[tail:, :] = jnp.zeros((plan.depth - tail, prod_ref.shape[1]), jnp.bfloat16)

    def vector(p, v):
        return got_ref[p, :, v].reshape(plan.wide, LANES)

    def one_plane(p, carry):
        after = lax.rem(p + 1, planes)
        before = lax.rem(p + planes - 1, planes)
        center = jnp.concatenate([vector(p, v) for v in range(plan.vectors)], axis=1)
        along_x = [
            (0.5 * (vector(after, v).astype(jnp.float32) - vector(before, v).astype(jnp.float32))).astype(jnp.bfloat16)
            for v in range(inner)
        ]
        along_yz = jnp.dot(center, stencil_ref[...], preferred_element_type=jnp.float32).astype(jnp.bfloat16)
        fields = jnp.concatenate([center[:, : inner * LANES]] + along_x + [along_yz], axis=1)
        field_ref[...] = jnp.dot(pick, fields, preferred_element_type=jnp.float32)

        def part(rows, which, v):
            at = (which * inner + v) * LANES
            return field_ref[rows, at : at + LANES]

        for v in range(inner):
            moving = [part(slice(d * pad, d * pad + plan.main), 0, v) for d in range(COMPS)]
            for c in range(COMPS):
                lanes = slice((v * COMPS + c) * LANES, (v * COMPS + c + 1) * LANES)
                for j in range(plan.modes):
                    at = slice(c * pad + j, c * pad + j + 1)
                    term = moving[0] * part(at, 1, v)
                    for d in range(1, COMPS):
                        term = term + moving[d] * part(at, 1 + d, v)
                    prod_ref[j * plan.main : (j + 1) * plan.main, lanes] = term.astype(jnp.bfloat16)
                if plan.rest:
                    slope = [part(slice(c * pad, (c + 1) * pad), 1 + d, v) for d in range(COMPS)]
                    terms = []
                    for i in range(plan.main, plan.modes):
                        term = part(slice(i, i + 1), 0, v) * slope[0]
                        for d in range(1, COMPS):
                            term = term + part(slice(d * pad + i, d * pad + i + 1), 0, v) * slope[d]
                        terms.append(term)
                    spare = plan.rest_rows - plan.rest * pad
                    if spare:
                        terms.append(jnp.zeros((spare, LANES), jnp.float32))
                    prod_ref[plan.pairs : tail, lanes] = jnp.concatenate(terms, axis=0).astype(jnp.bfloat16)
        total = jnp.dot(table_ref[0], prod_ref[0:TILE, :], preferred_element_type=jnp.float32)
        for g in range(1, plan.groups):
            total = total + jnp.dot(
                table_ref[g], prod_ref[g * TILE : (g + 1) * TILE, :], preferred_element_type=jnp.float32
            )
        for v in range(inner):
            stacked = jnp.concatenate(
                [total[:, (v * COMPS + c) * LANES : (v * COMPS + c + 1) * LANES] for c in range(COMPS)], axis=0
            )
            placed = jnp.dot(place, stacked.astype(jnp.bfloat16), preferred_element_type=jnp.float32)
            out_ref[p, :, v] = placed.astype(jnp.bfloat16).reshape(plan.chunks, plan.packed, LANES)
        return carry

    lax.fori_loop(0, planes, one_plane, 0)


def finish_kernel(plan, got_ref, base_ref, conv_ref, next_ref, flat_ref):
    for chunk in range(plan.chunks):
        for v in range(plan.inner):
            items = [got_ref[s, chunk, v].astype(jnp.float32) for s in range(plan.planes)]
            swapped = swap_blocks(items, plan.width)
            for block in range(min(plan.planes, plan.rows - v * plan.planes)):
                at = (chunk * plan.rows + v * plan.planes + block) * plan.packed
                flat_ref[at : at + plan.packed, :] = swapped[block]
    for f in range(plan.fields):
        value = flat_ref[pl.ds(f, plan.ny, stride=plan.packed), :]
        conv_ref[f] = value
        next_ref[f] = base_ref[f] - SECTION_STEP * value


def on_device(velocity, base_velocity, mode_slot, triples, triple_coef):
    slot_dev, _, _, ny, nz = velocity.shape
    chunks, planes = lax.axis_size("chaos"), lax.axis_size("space")
    plan = Plan(slot_dev, ny, nz, planes, chunks, mode_slot.shape[0])
    fields, packed, devices = plan.fields, plan.packed, planes * chunks

    def exchange(block):
        flat = block.reshape((devices,) + block.shape[2:])
        return lax.all_to_all(flat, ("space", "chaos"), 0, 0, tiled=True).reshape(block.shape)

    sent = pl.pallas_call(
        functools.partial(pack_kernel, plan),
        out_shape=jax.ShapeDtypeStruct((planes, chunks, plan.vectors, packed, LANES), jnp.bfloat16),
        in_specs=[vmem_spec()],
        out_specs=vmem_spec(),
        compiler_params=params(),
        name="pack",
    )(velocity.reshape(fields * ny, nz))
    got = exchange(sent)
    table = pl.pallas_call(
        functools.partial(table_kernel, plan),
        out_shape=jax.ShapeDtypeStruct((plan.groups, plan.mode_pad, TILE), jnp.bfloat16),
        in_specs=[vmem_spec(), vmem_spec()],
        out_specs=vmem_spec(),
        compiler_params=params(),
        name="table",
    )(triples.T, triple_coef.reshape(1, -1))
    returned = pl.pallas_call(
        functools.partial(contract_kernel, plan),
        out_shape=jax.ShapeDtypeStruct((planes, chunks, plan.inner, packed, LANES), jnp.bfloat16),
        in_specs=[pl.BlockSpec(memory_space=pltpu.SMEM)] + [vmem_spec()] * 3,
        out_specs=vmem_spec(),
        scratch_shapes=[
            pltpu.VMEM((COMPS * plan.mode_pad, 4 * plan.inner * LANES), jnp.float32),
            pltpu.VMEM((plan.depth, COMPS * plan.inner * LANES), jnp.bfloat16),
        ],
        compiler_params=params(),
        name="contract",
    )(mode_slot, got, jnp.asarray(plan.stencil(), jnp.bfloat16), table)
    convection, next_velocity = pl.pallas_call(
        functools.partial(finish_kernel, plan),
        out_shape=[jax.ShapeDtypeStruct((fields, ny, nz), jnp.float32)] * 2,
        in_specs=[vmem_spec(), vmem_spec()],
        out_specs=[vmem_spec(), vmem_spec()],
        scratch_shapes=[pltpu.VMEM((ny * packed, LANES), jnp.float32)],
        compiler_params=params(),
        name="finish",
    )(exchange(returned), base_velocity.reshape(fields, ny, nz))
    return convection.reshape(velocity.shape), next_velocity.reshape(velocity.shape)


def solution(mesh):
    spread = P("chaos", None, "space", None, None)
    return jax.shard_map(
        on_device,
        mesh=mesh,
        in_specs=(spread, spread, P(), P(), P()),
        out_specs=(spread, spread),
        check_vma=False,
    )
```

```python
import functools

import jax
import jax.numpy as jnp
from jax import lax
from jax.experimental import pallas as pl
from jax.experimental.pallas import tpu as pltpu
from jax.sharding import PartitionSpec as P

SECTION_STEP = 0.5
COMPS = 3
LANES = 128
TILE = 256
STEP_ROWS = 2
VMEM_LIMIT = 48 * 1024 * 1024


def round_up(value, unit):
    return -(-value // unit) * unit


def vmem_specs(count):
    return [pl.BlockSpec(memory_space=pltpu.VMEM)] * count


def smem_spec():
    return pl.BlockSpec(memory_space=pltpu.SMEM)


def params():
    return pltpu.CompilerParams(vmem_limit_bytes=VMEM_LIMIT)


class Plan:
    def __init__(self, slot_dev, ny, nz, chunks, modes):
        self.slot_dev, self.ny, self.chunks, self.modes = slot_dev, ny, chunks, modes
        self.fields = slot_dev * COMPS
        self.packed = round_up(self.fields, 16)
        self.wide = chunks * self.packed
        self.rows = ny // chunks
        assert nz == LANES and self.rows * chunks == ny and self.rows % STEP_ROWS == 0
        assert chunks & (chunks - 1) == 0
        self.pad = round_up(modes, 8)
        self.main = modes // 16 * 16
        self.rest = modes - self.main
        self.rest_rows = round_up(self.rest * self.pad, 16)
        self.pairs = modes * self.main
        self.tail = self.pairs + self.rest_rows
        self.depth = round_up(self.tail, TILE)
        self.groups = self.depth // TILE


def pack_kernel(plan, me_ref, v_ref, *out_refs):
    rows, ny = plan.rows, plan.ny
    pad = jnp.zeros((plan.packed - plan.fields, LANES), jnp.float32)
    for k in range(plan.chunks):
        first = (me_ref[0] ^ k) * rows + ny - 1
        for r in range(rows + 2):
            block = v_ref[pl.ds(lax.rem(first + r, ny), plan.fields, stride=ny), :]
            out_refs[k][r] = jnp.concatenate([block, pad], axis=0).astype(jnp.bfloat16)


def merge_kernel(plan, *refs):
    out_ref = refs[-1]
    for k in range(plan.chunks):
        out_ref[k] = refs[k][1 : plan.rows + 1]


def table_kernel(plan, triples_ref, coef_ref, out_ref):
    count = triples_ref.shape[1]
    mode_i = triples_ref[0:1, :]
    mode_j = triples_ref[1:2, :]
    mode_k = triples_ref[2:3, :]
    place = jnp.where(
        mode_i < plan.main,
        mode_j * plan.main + mode_i,
        plan.pairs + (mode_i - plan.main) * plan.pad + mode_j,
    )
    row = (place // TILE) * plan.pad + mode_k
    column = place % TILE
    coef = coef_ref[...].astype(jnp.float32)
    height = plan.groups * plan.pad
    total = jnp.zeros((height, TILE), jnp.float32)
    step = 1024 if count % 1024 == 0 else count
    row_iota = lax.broadcasted_iota(jnp.int32, (height, step), 0)
    column_iota = lax.broadcasted_iota(jnp.int32, (TILE, step), 0)
    for start in range(0, count, step):
        part = slice(start, start + step)
        left = jnp.where(row_iota == row[:, part], coef[:, part], 0.0).astype(jnp.bfloat16)
        right = jnp.where(column_iota == column[:, part], 1.0, 0.0).astype(jnp.bfloat16)
        total = total + lax.dot_general(
            left, right, (((1,), (1,)), ((), ())), preferred_element_type=jnp.float32
        )
    for g in range(plan.groups):
        out_ref[g] = total[g * plan.pad : (g + 1) * plan.pad].astype(jnp.bfloat16)


def mode_picker(plan, me_ref, slot_ref):
    shape = (plan.pad, plan.wide)
    column = lax.broadcasted_iota(jnp.int32, shape, 1)
    mode = lax.broadcasted_iota(jnp.int32, shape, 0)
    inner = column % plan.packed
    owner = (column // plan.packed) ^ me_ref[0]
    slot = jnp.where(inner < plan.fields, owner * plan.slot_dev + inner // COMPS, -1)
    wanted = jnp.full(shape, -2, jnp.int32)
    for m in range(plan.modes):
        wanted = jnp.where(mode == m, slot_ref[m], wanted)
    hit = jnp.where(wanted == slot, 1.0, 0.0)
    return jnp.concatenate([jnp.where(inner % COMPS == d, hit, 0.0) for d in range(COMPS)], axis=0)


def clear_tail(plan, prod_ref):
    if plan.tail < plan.depth:
        prod_ref[plan.tail :, :] = jnp.zeros((plan.depth - plan.tail, prod_ref.shape[1]), jnp.bfloat16)


def contract(plan, table_ref, prod_ref):
    total = jnp.dot(table_ref[0], prod_ref[0:TILE, :], preferred_element_type=jnp.float32)
    for g in range(1, plan.groups):
        total = total + jnp.dot(
            table_ref[g], prod_ref[g * TILE : (g + 1) * TILE, :], preferred_element_type=jnp.float32
        )
    return total


def inplane_kernel(plan, me_ref, slot_ref, *refs):
    got_refs = refs[: plan.chunks]
    table_ref, out_ref, field_ref, prod_ref = refs[plan.chunks :]
    pad = plan.pad
    pick = mode_picker(plan, me_ref, slot_ref).astype(jnp.bfloat16)
    source = lax.broadcasted_iota(jnp.int32, (LANES, LANES), 0)
    target = lax.broadcasted_iota(jnp.int32, (LANES, LANES), 1)
    ahead = jnp.where(source == (target + 1) % LANES, 0.5, 0.0)
    behind = jnp.where(source == (target + LANES - 1) % LANES, 0.5, 0.0)
    stencil = (ahead - behind).astype(jnp.bfloat16)
    clear_tail(plan, prod_ref)

    def some_rows(step, carry):
        first = step * STEP_ROWS
        lines = [
            jnp.concatenate([ref[first + r] for ref in got_refs], axis=0) for r in range(STEP_ROWS + 2)
        ]
        wide_lines = [line.astype(jnp.float32) for line in lines]
        parts = []
        for r in range(STEP_ROWS):
            along_y = (0.5 * (wide_lines[r + 2] - wide_lines[r])).astype(jnp.bfloat16)
            along_z = jnp.dot(lines[r + 1], stencil, preferred_element_type=jnp.float32).astype(jnp.bfloat16)
            parts += [lines[r + 1], along_y, along_z]
        field_ref[...] = jnp.dot(pick, jnp.concatenate(parts, axis=1), preferred_element_type=jnp.float32)
        for r in range(STEP_ROWS):

            def part(rows, which):
                at = (r * 3 + which) * LANES
                return field_ref[rows, at : at + LANES]

            def line(row, which):
                return part(slice(row, row + 1), which)

            moving = [part(slice(d * pad, d * pad + plan.main), 0) for d in (1, 2)]
            for c in range(COMPS):
                lanes = slice((r * COMPS + c) * LANES, (r * COMPS + c + 1) * LANES)
                for j in range(plan.modes):
                    term = moving[0] * line(c * pad + j, 1) + moving[1] * line(c * pad + j, 2)
                    prod_ref[j * plan.main : (j + 1) * plan.main, lanes] = term.astype(jnp.bfloat16)
                if plan.rest:
                    slope = [part(slice(c * pad, (c + 1) * pad), d) for d in (1, 2)]
                    terms = [
                        line(pad + i, 0) * slope[0] + line(2 * pad + i, 0) * slope[1]
                        for i in range(plan.main, plan.modes)
                    ]
                    if plan.rest_rows > plan.rest * pad:
                        terms.append(jnp.zeros((plan.rest_rows - plan.rest * pad, LANES), jnp.float32))
                    prod_ref[plan.pairs : plan.tail, lanes] = jnp.concatenate(terms, axis=0).astype(jnp.bfloat16)
        out_ref[step] = contract(plan, table_ref, prod_ref)
        return carry

    lax.fori_loop(0, plan.rows // STEP_ROWS, some_rows, 0)


def crossplane_kernel(plan, me_ref, slot_ref, center_ref, low_ref, high_ref, table_ref, begun_ref, *refs):
    out_refs = refs[: plan.chunks]
    field_ref, prod_ref = refs[plan.chunks :]
    pad = plan.pad
    picker = mode_picker(plan, me_ref, slot_ref)
    pick = picker.astype(jnp.bfloat16)
    place = picker.T.astype(jnp.bfloat16)
    clear_tail(plan, prod_ref)

    def some_rows(step, carry):
        first = step * STEP_ROWS

        def raw(ref, r):
            return ref[:, first + r].reshape(plan.wide, LANES)

        parts = []
        for r in range(STEP_ROWS):
            along_x = 0.5 * (raw(high_ref, r).astype(jnp.float32) - raw(low_ref, r).astype(jnp.float32))
            parts += [raw(center_ref, r), along_x.astype(jnp.bfloat16)]
        field_ref[...] = jnp.dot(pick, jnp.concatenate(parts, axis=1), preferred_element_type=jnp.float32)
        for r in range(STEP_ROWS):

            def part(rows, which):
                at = (r * 2 + which) * LANES
                return field_ref[rows, at : at + LANES]

            def line(row, which):
                return part(slice(row, row + 1), which)

            moving = part(slice(0, plan.main), 0).astype(jnp.bfloat16)
            for c in range(COMPS):
                lanes = slice((r * COMPS + c) * LANES, (r * COMPS + c + 1) * LANES)
                for j in range(plan.modes):
                    slope = jnp.broadcast_to(line(c * pad + j, 1), (16, LANES)).astype(jnp.bfloat16)
                    for i in range(0, plan.main, 16):
                        prod_ref[j * plan.main + i : j * plan.main + i + 16, lanes] = moving[i : i + 16] * slope
                if plan.rest:
                    slope = part(slice(c * pad, (c + 1) * pad), 1)
                    terms = [line(i, 0) * slope for i in range(plan.main, plan.modes)]
                    if plan.rest_rows > plan.rest * pad:
                        terms.append(jnp.zeros((plan.rest_rows - plan.rest * pad, LANES), jnp.float32))
                    prod_ref[plan.pairs : plan.tail, lanes] = jnp.concatenate(terms, axis=0).astype(jnp.bfloat16)
        total = begun_ref[step] + contract(plan, table_ref, prod_ref)
        for r in range(STEP_ROWS):
            stacked = jnp.concatenate(
                [total[:, (r * COMPS + c) * LANES : (r * COMPS + c + 1) * LANES] for c in range(COMPS)], axis=0
            )
            placed = jnp.dot(place, stacked.astype(jnp.bfloat16), preferred_element_type=jnp.float32)
            placed = placed.astype(jnp.bfloat16)
            for k in range(plan.chunks):
                out_refs[k][first + r] = placed[k * plan.packed : (k + 1) * plan.packed]
        return carry

    lax.fori_loop(0, plan.rows // STEP_ROWS, some_rows, 0)


def finish_kernel(plan, me_ref, *refs):
    got_refs = refs[: plan.chunks]
    base_ref, conv_ref, next_ref, flat_ref = refs[plan.chunks :]
    for k in range(plan.chunks):
        first = (me_ref[0] ^ k) * plan.rows
        for r in range(plan.rows):
            at = pl.multiple_of((first + r) * plan.packed, plan.packed)
            flat_ref[pl.ds(at, plan.packed), :] = got_refs[k][r].astype(jnp.float32)
    for f in range(plan.fields):
        value = flat_ref[pl.ds(f, plan.ny, stride=plan.packed), :]
        conv_ref[f] = value
        next_ref[f] = base_ref[f] - SECTION_STEP * value


def on_device(velocity, base_velocity, mode_slot, triples, triple_coef):
    slot_dev, _, _, ny, nz = velocity.shape
    chunks, planes = lax.axis_size("chaos"), lax.axis_size("space")
    plan = Plan(slot_dev, ny, nz, chunks, mode_slot.shape[0])
    fields, packed, rows = plan.fields, plan.packed, plan.rows
    me = lax.axis_index("chaos").astype(jnp.int32).reshape(1)

    def exchange(blocks):
        partners = [[(i, i ^ k) for i in range(chunks)] for k in range(chunks)]
        return [blocks[0]] + [lax.ppermute(blocks[k], "chaos", partners[k]) for k in range(1, chunks)]

    sent = pl.pallas_call(
        functools.partial(pack_kernel, plan),
        out_shape=[jax.ShapeDtypeStruct((rows + 2, packed, nz), jnp.bfloat16)] * chunks,
        in_specs=[smem_spec()] + vmem_specs(1),
        out_specs=vmem_specs(chunks),
        compiler_params=params(),
        name="pack",
    )(me, velocity.reshape(fields * ny, nz))
    got = exchange(sent)
    center = pl.pallas_call(
        functools.partial(merge_kernel, plan),
        out_shape=jax.ShapeDtypeStruct((chunks, rows, packed, nz), jnp.bfloat16),
        in_specs=vmem_specs(chunks),
        out_specs=vmem_specs(1)[0],
        compiler_params=params(),
        name="merge",
    )(*got)
    forward = [(i, (i + 1) % planes) for i in range(planes)]
    backward = [(target, source) for source, target in forward]
    low = lax.ppermute(center, "space", forward)
    high = lax.ppermute(center, "space", backward)
    table = pl.pallas_call(
        functools.partial(table_kernel, plan),
        out_shape=jax.ShapeDtypeStruct((plan.groups, plan.pad, TILE), jnp.bfloat16),
        in_specs=vmem_specs(2),
        out_specs=vmem_specs(1)[0],
        compiler_params=params(),
        name="table",
    )(triples.T, triple_coef.reshape(1, -1))
    wide_step = STEP_ROWS * COMPS * LANES
    begun = pl.pallas_call(
        functools.partial(inplane_kernel, plan),
        out_shape=jax.ShapeDtypeStruct((rows // STEP_ROWS, plan.pad, wide_step), jnp.float32),
        in_specs=[smem_spec()] * 2 + vmem_specs(chunks + 1),
        out_specs=vmem_specs(1)[0],
        scratch_shapes=[
            pltpu.VMEM((COMPS * plan.pad, STEP_ROWS * 3 * LANES), jnp.float32),
            pltpu.VMEM((plan.depth, wide_step), jnp.bfloat16),
        ],
        compiler_params=params(),
        cost_estimate=pl.CostEstimate(flops=6_000_000_000, bytes_accessed=2_000_000, transcendentals=0),
        name="inplane",
    )(me, mode_slot, *got, table)
    returned = pl.pallas_call(
        functools.partial(crossplane_kernel, plan),
        out_shape=[jax.ShapeDtypeStruct((rows, packed, nz), jnp.bfloat16)] * chunks,
        in_specs=[smem_spec()] * 2 + vmem_specs(5),
        out_specs=vmem_specs(chunks),
        scratch_shapes=[
            pltpu.VMEM((COMPS * plan.pad, STEP_ROWS * 2 * LANES), jnp.float32),
            pltpu.VMEM((plan.depth, wide_step), jnp.bfloat16),
        ],
        compiler_params=params(),
        name="crossplane",
    )(me, mode_slot, center, low, high, table, begun)
    convection, next_velocity = pl.pallas_call(
        functools.partial(finish_kernel, plan),
        out_shape=[jax.ShapeDtypeStruct((fields, ny, nz), jnp.float32)] * 2,
        in_specs=[smem_spec()] + vmem_specs(chunks + 1),
        out_specs=vmem_specs(2),
        scratch_shapes=[pltpu.VMEM((ny * packed, LANES), jnp.float32)],
        compiler_params=params(),
        name="finish",
    )(me, *exchange(returned), base_velocity.reshape(fields, ny, nz))
    return convection.reshape(velocity.shape), next_velocity.reshape(velocity.shape)


def solution(mesh):
    spread = P("chaos", None, "space", None, None)
    return jax.shard_map(
        on_device,
        mesh=mesh,
        in_specs=(spread, spread, P(), P(), P()),
        out_specs=(spread, spread),
        check_vma=False,
    )
```

```python
import functools

import jax
import jax.numpy as jnp
import numpy as np
from jax import lax
from jax.experimental import pallas as pl
from jax.experimental.pallas import tpu as pltpu
from jax.sharding import PartitionSpec as P

SECTION_STEP = 0.5
COMPS = 3
LANES = 128
LANE_BITS = 7
TILE = 256
VMEM_LIMIT = 48 * 1024 * 1024


def round_up(value, unit):
    return -(-value // unit) * unit


def vmem_spec():
    return pl.BlockSpec(memory_space=pltpu.VMEM)


def params():
    return pltpu.CompilerParams(vmem_limit_bytes=VMEM_LIMIT)


class Plan:
    def __init__(self, slot_dev, ny, nz, planes, chunks, modes):
        self.slot_dev, self.ny, self.planes, self.chunks, self.modes = slot_dev, ny, planes, chunks, modes
        self.fields = slot_dev * COMPS
        self.packed = round_up(self.fields, 16)
        self.wide = chunks * self.packed
        self.rows = ny // chunks
        self.width = nz // planes
        assert nz == LANES and self.width * planes == nz and self.rows * chunks == ny
        self.width_bits = self.width.bit_length() - 1
        assert planes & (planes - 1) == 0 and 2 * self.rows <= self.width
        self.inner = -(-self.rows // planes)
        if self.rows % planes == 0:
            assert planes >= 3
            self.vectors = self.inner + 1
            first = self.inner * planes
            self.low, self.high, self.side = first, first + 1, first + 2
        else:
            assert self.rows + 3 <= planes
            self.vectors = 1
            self.low, self.high, self.side = planes - 1, self.rows, self.rows + 1
        self.mode_pad = round_up(modes, 8)
        self.main = modes // 16 * 16
        self.rest = modes - self.main
        self.rest_rows = round_up(self.rest * self.mode_pad, 16)
        self.pairs = modes * self.main
        self.depth = round_up(self.pairs + self.rest_rows, TILE)
        self.groups = self.depth // TILE
        work = [(v, c) for v in range(self.inner) for c in range(COMPS)]
        self.tiles = [work[at : at + 2] for at in range(0, len(work), 2)]

    def stencil(self):
        out = np.zeros((self.vectors * LANES, 2 * self.inner * LANES), np.float32)
        width = self.width
        for r in range(self.rows):
            above = r + 1 if r + 1 < self.rows else self.high
            below = r - 1 if r > 0 else self.low
            for w in range(width):
                at = r * width + w
                out[above * width + w, at] += 0.5
                out[below * width + w, at] -= 0.5
                right = at + 1 if w + 1 < width else self.side * width + 2 * r + 1
                left = at - 1 if w > 0 else self.side * width + 2 * r
                out[right, self.inner * LANES + at] += 0.5
                out[left, self.inner * LANES + at] -= 0.5
        return out


def block_transposer(plan):
    size = plan.planes * LANES
    source = lax.broadcasted_iota(jnp.int32, (size, size), 0)
    target = lax.broadcasted_iota(jnp.int32, (size, size), 1)
    part, lane = source >> LANE_BITS, source & (LANES - 1)
    block, inner = lane >> plan.width_bits, lane & (plan.width - 1)
    wanted = (block << LANE_BITS) + (part << plan.width_bits) + inner
    return jnp.where(target == wanted, 1.0, 0.0).astype(jnp.bfloat16)


def side_collector(plan):
    source = lax.broadcasted_iota(jnp.int32, (plan.rows * LANES, LANES), 0)
    target = lax.broadcasted_iota(jnp.int32, (plan.rows * LANES, LANES), 1)
    block, inner = target >> plan.width_bits, target & (plan.width - 1)
    beside = (block << plan.width_bits) - 1 + (inner & 1) * (plan.width + 1)
    wanted = ((inner >> 1) << LANE_BITS) + (beside & (LANES - 1))
    return jnp.where((source == wanted) & (inner < 2 * plan.rows), 1.0, 0.0).astype(jnp.bfloat16)


def pack_kernel(plan, v_ref, out_ref):
    planes, rows, chunks, packed = plan.planes, plan.rows, plan.chunks, plan.packed
    pad = jnp.zeros((packed - plan.fields, LANES), jnp.float32)
    lines = []
    for y in range(plan.ny):
        block = v_ref[pl.ds(y, plan.fields, stride=plan.ny), :]
        lines.append(jnp.concatenate([block, pad], axis=0).astype(jnp.bfloat16))

    def across(offset):
        return jnp.concatenate([lines[(c * rows + offset) % plan.ny] for c in range(chunks)], axis=0)

    transposer = block_transposer(plan)
    inside = [across(r) for r in range(rows)]
    side = jnp.dot(jnp.concatenate(inside, axis=1), side_collector(plan), preferred_element_type=jnp.float32)
    blocks = inside + [jnp.zeros_like(inside[0])] * (plan.vectors * planes - rows)
    blocks[plan.low] = across(-1)
    blocks[plan.high] = across(rows)
    blocks[plan.side] = side.astype(jnp.bfloat16)
    for v in range(plan.vectors):
        row = jnp.concatenate(blocks[v * planes : (v + 1) * planes], axis=1)
        swapped = jnp.dot(row, transposer, preferred_element_type=jnp.float32).astype(jnp.bfloat16)
        for s in range(planes):
            for c in range(chunks):
                out_ref[s, c, v] = swapped[c * packed : (c + 1) * packed, s * LANES : (s + 1) * LANES]


def table_kernel(plan, triples_ref, coef_ref, out_ref):
    count = triples_ref.shape[1]
    mode_i = triples_ref[0:1, :]
    mode_j = triples_ref[1:2, :]
    mode_k = triples_ref[2:3, :]
    place = jnp.where(
        mode_i < plan.main,
        mode_j * plan.main + mode_i,
        plan.pairs + (mode_i - plan.main) * plan.mode_pad + mode_j,
    )
    row = (place // TILE) * plan.mode_pad + mode_k
    column = place % TILE
    coef = coef_ref[...].astype(jnp.float32)
    height = plan.groups * plan.mode_pad
    total = jnp.zeros((height, TILE), jnp.float32)
    step = 1024 if count % 1024 == 0 else count
    row_iota = lax.broadcasted_iota(jnp.int32, (height, step), 0)
    column_iota = lax.broadcasted_iota(jnp.int32, (TILE, step), 0)
    for start in range(0, count, step):
        part = slice(start, start + step)
        left = jnp.where(row_iota == row[:, part], coef[:, part], 0.0).astype(jnp.bfloat16)
        right = jnp.where(column_iota == column[:, part], 1.0, 0.0).astype(jnp.bfloat16)
        total = total + lax.dot_general(
            left, right, (((1,), (1,)), ((), ())), preferred_element_type=jnp.float32
        )
    for g in range(plan.groups):
        out_ref[:, g * TILE : (g + 1) * TILE] = total[g * plan.mode_pad : (g + 1) * plan.mode_pad].astype(jnp.bfloat16)


def mode_picker(plan, slot_ref):
    shape = (plan.mode_pad, plan.wide)
    column = lax.broadcasted_iota(jnp.int32, shape, 1)
    mode = lax.broadcasted_iota(jnp.int32, shape, 0)
    inner = column % plan.packed
    slot = jnp.where(
        inner < plan.fields, (column // plan.packed) * plan.slot_dev + inner // COMPS, -1
    )
    wanted = jnp.full(shape, -2, jnp.int32)
    for m in range(plan.modes):
        wanted = jnp.where(mode == m, slot_ref[m], wanted)
    hit = jnp.where(wanted == slot, 1.0, 0.0)
    return jnp.concatenate([jnp.where(inner % COMPS == d, hit, 0.0) for d in range(COMPS)], axis=0)


def contract_kernel(plan, slot_ref, got_ref, stencil_ref, table_ref, out_ref, field_ref, conv_ref, *prod_refs):
    planes, inner, pad = plan.planes, plan.inner, plan.mode_pad
    picker = mode_picker(plan, slot_ref)
    pick = picker.astype(jnp.bfloat16)
    place = picker.T.astype(jnp.bfloat16)
    tail = plan.pairs + plan.rest_rows
    if tail < plan.depth:
        for ref in prod_refs:
            ref[tail:, :] = jnp.zeros((plan.depth - tail, ref.shape[1]), jnp.bfloat16)

    def vector(p, v):
        return got_ref[p % planes, :, v].reshape(plan.wide, LANES)

    for p in range(planes):
        center = jnp.concatenate([vector(p, v) for v in range(plan.vectors)], axis=1)
        along_x = [
            (0.5 * (vector(p + 1, v).astype(jnp.float32) - vector(p - 1, v).astype(jnp.float32))).astype(jnp.bfloat16)
            for v in range(inner)
        ]
        along_yz = jnp.dot(center, stencil_ref[...], preferred_element_type=jnp.float32).astype(jnp.bfloat16)
        fields = jnp.concatenate([center[:, : inner * LANES]] + along_x + [along_yz], axis=1)
        field_ref[p] = jnp.dot(pick, fields, preferred_element_type=jnp.float32)

    def fill(p, tile):
        for place_in_tile, (v, c) in enumerate(plan.tiles[tile]):
            prod_ref = prod_refs[tile]
            lanes = slice(place_in_tile * LANES, (place_in_tile + 1) * LANES)

            def part(rows, which):
                at = (which * inner + v) * LANES
                return field_ref[p, rows, at : at + LANES]

            moving = [part(slice(d * pad, d * pad + plan.main), 0) for d in range(COMPS)]
            for j in range(plan.modes):
                at = slice(c * pad + j, c * pad + j + 1)
                term = moving[0] * part(at, 1)
                for d in range(1, COMPS):
                    term = term + moving[d] * part(at, 1 + d)
                prod_ref[j * plan.main : (j + 1) * plan.main, lanes] = term.astype(jnp.bfloat16)
            if plan.rest:
                slope = [part(slice(c * pad, (c + 1) * pad), 1 + d) for d in range(COMPS)]
                terms = []
                for i in range(plan.main, plan.modes):
                    term = part(slice(i, i + 1), 0) * slope[0]
                    for d in range(1, COMPS):
                        term = term + part(slice(d * pad + i, d * pad + i + 1), 0) * slope[d]
                    terms.append(term)
                spare = plan.rest_rows - plan.rest * pad
                if spare:
                    terms.append(jnp.zeros((spare, LANES), jnp.float32))
                prod_ref[plan.pairs : tail, lanes] = jnp.concatenate(terms, axis=0).astype(jnp.bfloat16)

    def multiply(slot, tile):
        result = jnp.dot(table_ref[...], prod_refs[tile][...], preferred_element_type=jnp.float32)
        for place_in_tile, (v, c) in enumerate(plan.tiles[tile]):
            lanes = slice(place_in_tile * LANES, (place_in_tile + 1) * LANES)
            conv_ref[slot, v, c * pad : (c + 1) * pad, :] = result[:, lanes]

    last = len(plan.tiles) - 1

    def one_plane(p, carry):
        for tile in range(last + 1):
            if tile == 0:
                multiply(p, last)
            else:
                multiply(p + 1, tile - 1)
            fill(p, tile)
        return carry

    lax.fori_loop(0, planes, one_plane, 0)
    multiply(planes, last)
    for p in range(planes):
        stacked = jnp.concatenate([conv_ref[p + 1, v].astype(jnp.bfloat16) for v in range(inner)], axis=1)
        placed = jnp.dot(place, stacked, preferred_element_type=jnp.float32).astype(jnp.bfloat16)
        for v in range(inner):
            block = placed[:, v * LANES : (v + 1) * LANES]
            out_ref[p, :, v] = block.reshape(plan.chunks, plan.packed, LANES)


def finish_kernel(plan, got_ref, base_ref, conv_ref, next_ref, flat_ref):
    transposer = block_transposer(plan)
    for v in range(plan.inner):
        parts = [got_ref[s, :, v].reshape(plan.wide, LANES) for s in range(plan.planes)]
        swapped = jnp.dot(jnp.concatenate(parts, axis=1), transposer, preferred_element_type=jnp.float32)
        for block in range(min(plan.planes, plan.rows - v * plan.planes)):
            for chunk in range(plan.chunks):
                at = (chunk * plan.rows + v * plan.planes + block) * plan.packed
                flat_ref[at : at + plan.packed, :] = swapped[
                    chunk * plan.packed : (chunk + 1) * plan.packed, block * LANES : (block + 1) * LANES
                ]
    for f in range(plan.fields):
        value = flat_ref[pl.ds(f, plan.ny, stride=plan.packed), :]
        conv_ref[f] = value
        next_ref[f] = base_ref[f] - SECTION_STEP * value


def on_device(velocity, base_velocity, mode_slot, triples, triple_coef):
    slot_dev, _, _, ny, nz = velocity.shape
    chunks, planes = lax.axis_size("chaos"), lax.axis_size("space")
    plan = Plan(slot_dev, ny, nz, planes, chunks, mode_slot.shape[0])
    fields, packed, devices = plan.fields, plan.packed, planes * chunks

    def exchange(block):
        flat = block.reshape((devices,) + block.shape[2:])
        return lax.all_to_all(flat, ("space", "chaos"), 0, 0, tiled=True).reshape(block.shape)

    sent = pl.pallas_call(
        functools.partial(pack_kernel, plan),
        out_shape=jax.ShapeDtypeStruct((planes, chunks, plan.vectors, packed, LANES), jnp.bfloat16),
        in_specs=[vmem_spec()],
        out_specs=vmem_spec(),
        compiler_params=params(),
        name="pack",
    )(velocity.reshape(fields * ny, nz))
    got = exchange(sent)
    table = pl.pallas_call(
        functools.partial(table_kernel, plan),
        out_shape=jax.ShapeDtypeStruct((plan.mode_pad, plan.depth), jnp.bfloat16),
        in_specs=[vmem_spec(), vmem_spec()],
        out_specs=vmem_spec(),
        compiler_params=params(),
        name="table",
    )(triples.T, triple_coef.reshape(1, -1))
    returned = pl.pallas_call(
        functools.partial(contract_kernel, plan),
        out_shape=jax.ShapeDtypeStruct((planes, chunks, plan.inner, packed, LANES), jnp.bfloat16),
        in_specs=[pl.BlockSpec(memory_space=pltpu.SMEM)] + [vmem_spec()] * 3,
        out_specs=vmem_spec(),
        scratch_shapes=[
            pltpu.VMEM((planes, COMPS * plan.mode_pad, 4 * plan.inner * LANES), jnp.float32),
            pltpu.VMEM((planes + 1, plan.inner, COMPS * plan.mode_pad, LANES), jnp.float32),
        ]
        + [pltpu.VMEM((plan.depth, len(tile) * LANES), jnp.bfloat16) for tile in plan.tiles],
        compiler_params=params(),
        name="contract",
    )(mode_slot, got, jnp.asarray(plan.stencil(), jnp.bfloat16), table)
    convection, next_velocity = pl.pallas_call(
        functools.partial(finish_kernel, plan),
        out_shape=[jax.ShapeDtypeStruct((fields, ny, nz), jnp.float32)] * 2,
        in_specs=[vmem_spec(), vmem_spec()],
        out_specs=[vmem_spec(), vmem_spec()],
        scratch_shapes=[pltpu.VMEM((ny * packed, LANES), jnp.float32)],
        compiler_params=params(),
        name="finish",
    )(exchange(returned), base_velocity.reshape(fields, ny, nz))
    return convection.reshape(velocity.shape), next_velocity.reshape(velocity.shape)


def solution(mesh):
    spread = P("chaos", None, "space", None, None)
    return jax.shard_map(
        on_device,
        mesh=mesh,
        in_specs=(spread, spread, P(), P(), P()),
        out_specs=(spread, spread),
        check_vma=False,
    )
```

```python
import functools

import jax
import jax.numpy as jnp
import numpy as np
from jax import lax
from jax.experimental import pallas as pl
from jax.experimental.pallas import tpu as pltpu
from jax.sharding import PartitionSpec as P

SECTION_STEP = 0.5
COMPS = 3
LANES = 128
LANE_BITS = 7
TILE = 256
REPEAT = 8
VMEM_LIMIT = 48 * 1024 * 1024


def round_up(value, unit):
    return -(-value // unit) * unit


def vmem_spec():
    return pl.BlockSpec(memory_space=pltpu.VMEM)


def params():
    return pltpu.CompilerParams(vmem_limit_bytes=VMEM_LIMIT)


class Plan:
    def __init__(self, slot_dev, ny, nz, planes, chunks, modes):
        self.slot_dev, self.ny, self.planes, self.chunks, self.modes = slot_dev, ny, planes, chunks, modes
        self.fields = slot_dev * COMPS
        self.packed = round_up(self.fields, 16)
        self.wide = chunks * self.packed
        self.rows = ny // chunks
        self.width = nz // planes
        assert nz == LANES and self.width * planes == nz and self.rows * chunks == ny
        self.width_bits = self.width.bit_length() - 1
        assert planes & (planes - 1) == 0 and 2 * self.rows <= self.width
        self.inner = -(-self.rows // planes)
        if self.rows % planes == 0:
            assert planes >= 3
            self.vectors = self.inner + 1
            first = self.inner * planes
            self.low, self.high, self.side = first, first + 1, first + 2
        else:
            assert self.rows + 3 <= planes
            self.vectors = 1
            self.low, self.high, self.side = planes - 1, self.rows, self.rows + 1
        self.mode_pad = round_up(modes, 8)
        self.main = modes // 16 * 16
        self.rest = modes - self.main
        self.spread_rows = modes * COMPS * REPEAT
        self.rest_rows = round_up(self.rest * self.mode_pad, 16)
        self.pairs = modes * self.main
        self.depth = round_up(self.pairs + self.rest_rows, TILE)
        self.groups = self.depth // TILE
        self.lanes = self.inner * COMPS * LANES
        self.cuts = [(at, min(at + TILE, self.lanes)) for at in range(0, self.lanes, TILE)]

    def stencil(self):
        out = np.zeros((self.vectors * LANES, 2 * self.inner * LANES), np.float32)
        width = self.width
        for r in range(self.rows):
            above = r + 1 if r + 1 < self.rows else self.high
            below = r - 1 if r > 0 else self.low
            for w in range(width):
                at = r * width + w
                out[above * width + w, at] += 0.5
                out[below * width + w, at] -= 0.5
                right = at + 1 if w + 1 < width else self.side * width + 2 * r + 1
                left = at - 1 if w > 0 else self.side * width + 2 * r
                out[right, self.inner * LANES + at] += 0.5
                out[left, self.inner * LANES + at] -= 0.5
        return out


def block_transposer(plan):
    size = plan.planes * LANES
    source = lax.broadcasted_iota(jnp.int32, (size, size), 0)
    target = lax.broadcasted_iota(jnp.int32, (size, size), 1)
    part, lane = source >> LANE_BITS, source & (LANES - 1)
    block, inner = lane >> plan.width_bits, lane & (plan.width - 1)
    wanted = (block << LANE_BITS) + (part << plan.width_bits) + inner
    return jnp.where(target == wanted, 1.0, 0.0).astype(jnp.bfloat16)


def side_collector(plan):
    source = lax.broadcasted_iota(jnp.int32, (plan.rows * LANES, LANES), 0)
    target = lax.broadcasted_iota(jnp.int32, (plan.rows * LANES, LANES), 1)
    block, inner = target >> plan.width_bits, target & (plan.width - 1)
    beside = (block << plan.width_bits) - 1 + (inner & 1) * (plan.width + 1)
    wanted = ((inner >> 1) << LANE_BITS) + (beside & (LANES - 1))
    return jnp.where((source == wanted) & (inner < 2 * plan.rows), 1.0, 0.0).astype(jnp.bfloat16)


def pack_kernel(plan, v_ref, out_ref):
    planes, rows, chunks, packed = plan.planes, plan.rows, plan.chunks, plan.packed
    pad = jnp.zeros((packed - plan.fields, LANES), jnp.float32)
    lines = []
    for y in range(plan.ny):
        block = v_ref[pl.ds(y, plan.fields, stride=plan.ny), :]
        lines.append(jnp.concatenate([block, pad], axis=0).astype(jnp.bfloat16))

    def across(offset):
        return jnp.concatenate([lines[(c * rows + offset) % plan.ny] for c in range(chunks)], axis=0)

    transposer = block_transposer(plan)
    inside = [across(r) for r in range(rows)]
    side = jnp.dot(jnp.concatenate(inside, axis=1), side_collector(plan), preferred_element_type=jnp.float32)
    blocks = inside + [jnp.zeros_like(inside[0])] * (plan.vectors * planes - rows)
    blocks[plan.low] = across(-1)
    blocks[plan.high] = across(rows)
    blocks[plan.side] = side.astype(jnp.bfloat16)
    for v in range(plan.vectors):
        row = jnp.concatenate(blocks[v * planes : (v + 1) * planes], axis=1)
        swapped = jnp.dot(row, transposer, preferred_element_type=jnp.float32).astype(jnp.bfloat16)
        for s in range(planes):
            for c in range(chunks):
                out_ref[s, c, v] = swapped[c * packed : (c + 1) * packed, s * LANES : (s + 1) * LANES]


def prepare_kernel(plan, slot_ref, triples_ref, coef_ref, table_ref, spread_ref, place_ref, swap_ref):
    count = triples_ref.shape[1]
    mode_i = triples_ref[0:1, :]
    mode_j = triples_ref[1:2, :]
    mode_k = triples_ref[2:3, :]
    place = jnp.where(
        mode_j < plan.main,
        mode_i * plan.main + mode_j,
        plan.pairs + (mode_j - plan.main) * plan.mode_pad + mode_i,
    )
    row = (place // TILE) * plan.mode_pad + mode_k
    column = place % TILE
    coef = coef_ref[...].astype(jnp.float32)
    height = plan.groups * plan.mode_pad
    total = jnp.zeros((height, TILE), jnp.float32)
    step = 1024 if count % 1024 == 0 else count
    row_iota = lax.broadcasted_iota(jnp.int32, (height, step), 0)
    column_iota = lax.broadcasted_iota(jnp.int32, (TILE, step), 0)
    for start in range(0, count, step):
        part = slice(start, start + step)
        left = jnp.where(row_iota == row[:, part], coef[:, part], 0.0).astype(jnp.bfloat16)
        right = jnp.where(column_iota == column[:, part], 1.0, 0.0).astype(jnp.bfloat16)
        total = total + lax.dot_general(
            left, right, (((1,), (1,)), ((), ())), preferred_element_type=jnp.float32
        )
    for g in range(plan.groups):
        table_ref[:, g * TILE : (g + 1) * TILE] = total[g * plan.mode_pad : (g + 1) * plan.mode_pad].astype(jnp.bfloat16)

    shape = (plan.mode_pad, plan.wide)
    column = lax.broadcasted_iota(jnp.int32, shape, 1)
    mode = lax.broadcasted_iota(jnp.int32, shape, 0)
    inner = column % plan.packed
    slot = jnp.where(
        inner < plan.fields, (column // plan.packed) * plan.slot_dev + inner // COMPS, -1
    )
    wanted = jnp.full(shape, -2, jnp.int32)
    for m in range(plan.modes):
        wanted = jnp.where(mode == m, slot_ref[m], wanted)
    hit = jnp.where(wanted == slot, 1.0, 0.0)
    pickers = [jnp.where(inner % COMPS == d, hit, 0.0) for d in range(COMPS)]
    picker = jnp.concatenate(pickers, axis=0)
    place_ref[...] = picker.T.astype(jnp.bfloat16)
    for m in range(plan.modes):
        for d in range(0, COMPS):
            at = (m * COMPS + d) * REPEAT
            spread_ref[at : at + REPEAT] = jnp.broadcast_to(pickers[d][m : m + 1], (REPEAT, plan.wide))
    spread_ref[plan.spread_rows :] = picker
    swap_ref[...] = block_transposer(plan)


def contract_kernel(plan, got_ref, stencil_ref, table_ref, spread_ref, place_ref, out_ref, *scratch):
    repeat_ref, mode_ref, slope_ref, conv_ref, even_ref, odd_ref = scratch
    planes, inner, pad, main = plan.planes, plan.inner, plan.mode_pad, plan.main
    spread = spread_ref[...].astype(jnp.bfloat16)
    pick = spread[plan.spread_rows :]
    tail = plan.pairs + plan.rest_rows
    if tail < plan.depth:
        for ref in (even_ref, odd_ref):
            ref[tail:, :] = jnp.zeros((plan.depth - tail, ref.shape[1]), jnp.bfloat16)

    def vector(p, v):
        return got_ref[p % planes, :, v].reshape(plan.wide, LANES)

    for p in range(planes):
        center = jnp.concatenate([vector(p, v) for v in range(plan.vectors)], axis=1)
        along_x = [
            (0.5 * (vector(p + 1, v).astype(jnp.float32) - vector(p - 1, v).astype(jnp.float32))).astype(jnp.bfloat16)
            for v in range(inner)
        ]
        along_yz = jnp.dot(center, stencil_ref[...], preferred_element_type=jnp.float32).astype(jnp.bfloat16)
        moving = jnp.dot(spread, center[:, : inner * LANES], preferred_element_type=jnp.float32)
        repeat_ref[p] = moving[: plan.spread_rows]
        mode_ref[p] = moving[plan.spread_rows :]
        slopes = jnp.concatenate(along_x + [along_yz], axis=1)
        slope_ref[p] = jnp.dot(pick, slopes, preferred_element_type=jnp.float32)

    def fill(prod_ref, p, v):
        here = slice(v * LANES, (v + 1) * LANES)

        def slope(rows, d):
            at = (d * inner + v) * LANES
            return slope_ref[p, rows, at : at + LANES]

        def lanes(c):
            return slice((v * COMPS + c) * LANES, (v * COMPS + c + 1) * LANES)

        slopes = [[slope(slice(c * pad, c * pad + main), d) for d in range(COMPS)] for c in range(COMPS)]
        for i in range(plan.modes):
            moving = []
            for d in range(COMPS):
                at = (i * COMPS + d) * REPEAT
                one = repeat_ref[p, at : at + REPEAT, here]
                moving.append(jnp.concatenate([one] * (main // REPEAT), axis=0))
            for c in range(COMPS):
                term = moving[0] * slopes[c][0]
                for d in range(1, COMPS):
                    term = term + moving[d] * slopes[c][d]
                prod_ref[i * main : (i + 1) * main, lanes(c)] = term.astype(jnp.bfloat16)
        if plan.rest:
            moving = [mode_ref[p, d * pad : (d + 1) * pad, here] for d in range(COMPS)]
            for c in range(COMPS):
                terms = []
                for j in range(main, plan.modes):
                    at = slice(c * pad + j, c * pad + j + 1)
                    term = moving[0] * slope(at, 0)
                    for d in range(1, COMPS):
                        term = term + moving[d] * slope(at, d)
                    terms.append(term)
                spare = plan.rest_rows - plan.rest * pad
                if spare:
                    terms.append(jnp.zeros((spare, LANES), jnp.float32))
                prod_ref[plan.pairs : tail, lanes(c)] = jnp.concatenate(terms, axis=0).astype(jnp.bfloat16)

    def multiply(slot, prod_ref, cut):
        low, high = cut
        result = jnp.dot(table_ref[...], prod_ref[:, low:high], preferred_element_type=jnp.float32)
        for at in range(low, high, LANES):
            v, c = divmod(at // LANES, COMPS)
            conv_ref[slot, v, c * pad : (c + 1) * pad, :] = result[:, at - low : at - low + LANES]

    def beside(prod_ref, p, done_ref, slot):
        cuts = list(plan.cuts)
        for v in range(inner):
            if cuts:
                multiply(slot, done_ref, cuts.pop(0))
            fill(prod_ref, p, v)
        for cut in cuts:
            multiply(slot, done_ref, cut)

    def two_planes(step, carry):
        p = 2 * step
        beside(even_ref, p, odd_ref, p)
        beside(odd_ref, p + 1, even_ref, p + 1)
        return carry

    lax.fori_loop(0, planes // 2, two_planes, 0)
    for cut in plan.cuts:
        multiply(planes, odd_ref, cut)
    for p in range(planes):
        stacked = jnp.concatenate([conv_ref[p + 1, v].astype(jnp.bfloat16) for v in range(inner)], axis=1)
        placed = jnp.dot(place_ref[...], stacked, preferred_element_type=jnp.float32).astype(jnp.bfloat16)
        for v in range(inner):
            block = placed[:, v * LANES : (v + 1) * LANES]
            out_ref[p, :, v] = block.reshape(plan.chunks, plan.packed, LANES)


def finish_kernel(plan, got_ref, base_ref, swap_ref, conv_ref, next_ref, flat_ref, conv_vmem, next_vmem, sems):
    for v in range(plan.inner):
        parts = [got_ref[s, :, v].reshape(plan.wide, LANES) for s in range(plan.planes)]
        swapped = jnp.dot(jnp.concatenate(parts, axis=1), swap_ref[...], preferred_element_type=jnp.float32)
        for block in range(min(plan.planes, plan.rows - v * plan.planes)):
            for chunk in range(plan.chunks):
                at = (chunk * plan.rows + v * plan.planes + block) * plan.packed
                flat_ref[at : at + plan.packed, :] = swapped[
                    chunk * plan.packed : (chunk + 1) * plan.packed, block * LANES : (block + 1) * LANES
                ]
    copies = []
    for s in range(plan.slot_dev):
        fields = slice(s * COMPS, (s + 1) * COMPS)
        for f in range(s * COMPS, (s + 1) * COMPS):
            value = flat_ref[pl.ds(f, plan.ny, stride=plan.packed), :]
            conv_vmem[f] = value
            next_vmem[f] = base_ref[f] - SECTION_STEP * value
        for which, (source, target) in enumerate(((conv_vmem, conv_ref), (next_vmem, next_ref))):
            copies.append(pltpu.make_async_copy(source.at[fields], target.at[fields], sems.at[which, s]))
            copies[-1].start()
    for copy in copies:
        copy.wait()


def on_device(velocity, base_velocity, mode_slot, triples, triple_coef):
    slot_dev, _, _, ny, nz = velocity.shape
    chunks, planes = lax.axis_size("chaos"), lax.axis_size("space")
    plan = Plan(slot_dev, ny, nz, planes, chunks, mode_slot.shape[0])
    fields, packed, devices = plan.fields, plan.packed, planes * chunks

    def exchange(block):
        flat = block.reshape((devices,) + block.shape[2:])
        return lax.all_to_all(flat, ("space", "chaos"), 0, 0, tiled=True).reshape(block.shape)

    sent = pl.pallas_call(
        functools.partial(pack_kernel, plan),
        out_shape=jax.ShapeDtypeStruct((planes, chunks, plan.vectors, packed, LANES), jnp.bfloat16),
        in_specs=[vmem_spec()],
        out_specs=vmem_spec(),
        compiler_params=params(),
        name="pack",
    )(velocity.reshape(fields * ny, nz))
    got = exchange(sent)
    table, spread, place, swap = pl.pallas_call(
        functools.partial(prepare_kernel, plan),
        out_shape=[
            jax.ShapeDtypeStruct((plan.mode_pad, plan.depth), jnp.bfloat16),
            jax.ShapeDtypeStruct((plan.spread_rows + COMPS * plan.mode_pad, plan.wide), jnp.float32),
            jax.ShapeDtypeStruct((plan.wide, COMPS * plan.mode_pad), jnp.bfloat16),
            jax.ShapeDtypeStruct((planes * LANES, planes * LANES), jnp.bfloat16),
        ],
        in_specs=[pl.BlockSpec(memory_space=pltpu.SMEM)] + [vmem_spec()] * 2,
        out_specs=[vmem_spec()] * 4,
        compiler_params=params(),
        name="prepare",
    )(mode_slot, triples.T, triple_coef.reshape(1, -1))
    returned = pl.pallas_call(
        functools.partial(contract_kernel, plan),
        out_shape=jax.ShapeDtypeStruct((planes, chunks, plan.inner, packed, LANES), jnp.bfloat16),
        in_specs=[vmem_spec()] * 5,
        out_specs=vmem_spec(),
        scratch_shapes=[
            pltpu.VMEM((planes, plan.spread_rows, plan.inner * LANES), jnp.float32),
            pltpu.VMEM((planes, COMPS * plan.mode_pad, plan.inner * LANES), jnp.float32),
            pltpu.VMEM((planes, COMPS * plan.mode_pad, plan.lanes), jnp.float32),
            pltpu.VMEM((planes + 1, plan.inner, COMPS * plan.mode_pad, LANES), jnp.float32),
            pltpu.VMEM((plan.depth, plan.lanes), jnp.bfloat16),
            pltpu.VMEM((plan.depth, plan.lanes), jnp.bfloat16),
        ],
        compiler_params=params(),
        name="contract",
    )(got, jnp.asarray(plan.stencil(), jnp.bfloat16), table, spread, place)
    convection, next_velocity = pl.pallas_call(
        functools.partial(finish_kernel, plan),
        out_shape=[jax.ShapeDtypeStruct((fields, ny, nz), jnp.float32)] * 2,
        in_specs=[vmem_spec()] * 3,
        out_specs=[pl.BlockSpec(memory_space=pl.ANY)] * 2,
        scratch_shapes=[
            pltpu.VMEM((ny * packed, LANES), jnp.float32),
            pltpu.VMEM((fields, ny, nz), jnp.float32),
            pltpu.VMEM((fields, ny, nz), jnp.float32),
            pltpu.SemaphoreType.DMA((2, slot_dev)),
        ],
        compiler_params=params(),
        name="finish",
    )(exchange(returned), base_velocity.reshape(fields, ny, nz), swap)
    return convection.reshape(velocity.shape), next_velocity.reshape(velocity.shape)


def solution(mesh):
    spread = P("chaos", None, "space", None, None)
    return jax.shard_map(
        on_device,
        mesh=mesh,
        in_specs=(spread, spread, P(), P(), P()),
        out_specs=(spread, spread),
        check_vma=False,
    )
```

```python
import functools

import jax
import jax.numpy as jnp
import numpy as np
from jax import lax
from jax.experimental import pallas as pl
from jax.experimental.pallas import tpu as pltpu
from jax.sharding import PartitionSpec as P

SECTION_STEP = 0.5
COMPS = 3
LANES = 128
LANE_BITS = 7
TILE = 256
PACK = 16
VMEM_LIMIT = 48 * 1024 * 1024


def round_up(value, unit):
    return -(-value // unit) * unit


def vmem_spec():
    return pl.BlockSpec(memory_space=pltpu.VMEM)


def params():
    return pltpu.CompilerParams(vmem_limit_bytes=VMEM_LIMIT)


class Plan:
    def __init__(self, slot_dev, ny, nz, planes, chunks, modes):
        self.slot_dev, self.ny, self.planes, self.chunks, self.modes = slot_dev, ny, planes, chunks, modes
        self.fields = slot_dev * COMPS
        self.packed = round_up(self.fields, 16)
        self.wide = chunks * self.packed
        self.rows = ny // chunks
        self.width = nz // planes
        assert nz == LANES and self.width * planes == nz and self.rows * chunks == ny
        self.width_bits = self.width.bit_length() - 1
        assert self.rest_fits(modes)
        assert planes & (planes - 1) == 0 and 2 * self.rows <= self.width
        self.inner = -(-self.rows // planes)
        if self.rows % planes == 0:
            assert planes >= 3
            self.vectors = self.inner + 1
            first = self.inner * planes
            self.low, self.high, self.side = first, first + 1, first + 2
        else:
            assert self.rows + 3 <= planes
            self.vectors = 1
            self.low, self.high, self.side = planes - 1, self.rows, self.rows + 1
        self.mode_pad = round_up(modes, 8)
        self.main = modes // 16 * 16
        self.rest = modes - self.main
        self.wide_pad = round_up(modes, PACK)
        self.rest_rows = self.rest * self.wide_pad
        self.pairs = modes * self.main
        self.depth = round_up(self.pairs + self.rest_rows, TILE)
        self.groups = self.depth // TILE
        self.lanes = self.inner * COMPS * LANES
        self.cuts = [(at, min(at + TILE, self.lanes)) for at in range(0, self.lanes, TILE)]

    @staticmethod
    def rest_fits(modes):
        return modes >= PACK and modes % PACK <= 8

    def stencil(self):
        out = np.zeros((self.vectors * LANES, 2 * self.inner * LANES), np.float32)
        width = self.width
        for r in range(self.rows):
            above = r + 1 if r + 1 < self.rows else self.high
            below = r - 1 if r > 0 else self.low
            for w in range(width):
                at = r * width + w
                out[above * width + w, at] += 0.5
                out[below * width + w, at] -= 0.5
                right = at + 1 if w + 1 < width else self.side * width + 2 * r + 1
                left = at - 1 if w > 0 else self.side * width + 2 * r
                out[right, self.inner * LANES + at] += 0.5
                out[left, self.inner * LANES + at] -= 0.5
        return out


def block_transposer(plan):
    size = plan.planes * LANES
    source = lax.broadcasted_iota(jnp.int32, (size, size), 0)
    target = lax.broadcasted_iota(jnp.int32, (size, size), 1)
    part, lane = source >> LANE_BITS, source & (LANES - 1)
    block, inner = lane >> plan.width_bits, lane & (plan.width - 1)
    wanted = (block << LANE_BITS) + (part << plan.width_bits) + inner
    return jnp.where(target == wanted, 1.0, 0.0).astype(jnp.bfloat16)


def side_collector(plan):
    source = lax.broadcasted_iota(jnp.int32, (plan.rows * LANES, LANES), 0)
    target = lax.broadcasted_iota(jnp.int32, (plan.rows * LANES, LANES), 1)
    block, inner = target >> plan.width_bits, target & (plan.width - 1)
    beside = (block << plan.width_bits) - 1 + (inner & 1) * (plan.width + 1)
    wanted = ((inner >> 1) << LANE_BITS) + (beside & (LANES - 1))
    return jnp.where((source == wanted) & (inner < 2 * plan.rows), 1.0, 0.0).astype(jnp.bfloat16)


def pack_kernel(plan, v_ref, out_ref):
    planes, rows, chunks, packed = plan.planes, plan.rows, plan.chunks, plan.packed
    pad = jnp.zeros((packed - plan.fields, LANES), jnp.float32)
    lines = []
    for y in range(plan.ny):
        block = v_ref[pl.ds(y, plan.fields, stride=plan.ny), :]
        lines.append(jnp.concatenate([block, pad], axis=0).astype(jnp.bfloat16))

    def across(offset):
        return jnp.concatenate([lines[(c * rows + offset) % plan.ny] for c in range(chunks)], axis=0)

    transposer = block_transposer(plan)
    inside = [across(r) for r in range(rows)]
    side = jnp.dot(jnp.concatenate(inside, axis=1), side_collector(plan), preferred_element_type=jnp.float32)
    blocks = inside + [jnp.zeros_like(inside[0])] * (plan.vectors * planes - rows)
    blocks[plan.low] = across(-1)
    blocks[plan.high] = across(rows)
    blocks[plan.side] = side.astype(jnp.bfloat16)
    for v in range(plan.vectors):
        row = jnp.concatenate(blocks[v * planes : (v + 1) * planes], axis=1)
        swapped = jnp.dot(row, transposer, preferred_element_type=jnp.float32).astype(jnp.bfloat16)
        for s in range(planes):
            for c in range(chunks):
                out_ref[s, c, v] = swapped[c * packed : (c + 1) * packed, s * LANES : (s + 1) * LANES]


def prepare_kernel(plan, slot_ref, triples_ref, coef_ref, table_ref, pick_ref, place_ref, swap_ref):
    count = triples_ref.shape[1]
    mode_i = triples_ref[0:1, :]
    mode_j = triples_ref[1:2, :]
    mode_k = triples_ref[2:3, :]
    place = jnp.where(
        mode_j < plan.main,
        mode_i * plan.main + mode_j,
        plan.pairs + (mode_j - plan.main) * plan.wide_pad + mode_i,
    )
    row = (place // TILE) * plan.mode_pad + mode_k
    column = place % TILE
    coef = coef_ref[...].astype(jnp.float32)
    height = plan.groups * plan.mode_pad
    total = jnp.zeros((height, TILE), jnp.float32)
    step = 1024 if count % 1024 == 0 else count
    row_iota = lax.broadcasted_iota(jnp.int32, (height, step), 0)
    column_iota = lax.broadcasted_iota(jnp.int32, (TILE, step), 0)
    for start in range(0, count, step):
        part = slice(start, start + step)
        left = jnp.where(row_iota == row[:, part], coef[:, part], 0.0).astype(jnp.bfloat16)
        right = jnp.where(column_iota == column[:, part], 1.0, 0.0).astype(jnp.bfloat16)
        total = total + lax.dot_general(
            left, right, (((1,), (1,)), ((), ())), preferred_element_type=jnp.float32
        )
    for g in range(plan.groups):
        table_ref[:, g * TILE : (g + 1) * TILE] = total[g * plan.mode_pad : (g + 1) * plan.mode_pad].astype(jnp.bfloat16)

    shape = (plan.wide_pad, plan.wide)
    column = lax.broadcasted_iota(jnp.int32, shape, 1)
    mode = lax.broadcasted_iota(jnp.int32, shape, 0)
    inner = column % plan.packed
    slot = jnp.where(
        inner < plan.fields, (column // plan.packed) * plan.slot_dev + inner // COMPS, -1
    )
    wanted = jnp.full(shape, -2, jnp.int32)
    for m in range(plan.modes):
        wanted = jnp.where(mode == m, slot_ref[m], wanted)
    hit = jnp.where(wanted == slot, 1.0, 0.0)
    pickers = [jnp.where(inner % COMPS == d, hit, 0.0) for d in range(COMPS)]
    pick_ref[...] = jnp.concatenate(pickers, axis=0).astype(jnp.bfloat16)
    narrow = jnp.concatenate([picker[: plan.mode_pad] for picker in pickers], axis=0)
    place_ref[...] = narrow.T.astype(jnp.bfloat16)
    swap_ref[...] = block_transposer(plan)


def contract_kernel(plan, got_ref, stencil_ref, table_ref, pick_ref, place_ref, out_ref, *scratch):
    moving_ref, row_ref, slope_ref, conv_ref, even_ref, odd_ref = scratch
    planes, inner, pad, main, wide = plan.planes, plan.inner, plan.mode_pad, plan.main, plan.wide_pad
    tail = plan.pairs + plan.rest_rows
    if tail < plan.depth:
        for ref in (even_ref, odd_ref):
            ref[tail:, :] = jnp.zeros((plan.depth - tail, ref.shape[1]), jnp.bfloat16)

    def vector(p, v):
        return got_ref[p % planes, :, v].reshape(plan.wide, LANES)

    for p in range(planes):
        center = jnp.concatenate([vector(p, v) for v in range(plan.vectors)], axis=1)
        along_x = [
            (0.5 * (vector(p + 1, v).astype(jnp.float32) - vector(p - 1, v).astype(jnp.float32))).astype(jnp.bfloat16)
            for v in range(inner)
        ]
        along_yz = jnp.dot(center, stencil_ref[...], preferred_element_type=jnp.float32).astype(jnp.bfloat16)
        moving = center[:, : inner * LANES]
        moving_ref[p] = jnp.dot(pick_ref[...], moving, preferred_element_type=jnp.float32)
        slopes = jnp.dot(
            pick_ref[...], jnp.concatenate(along_x + [along_yz], axis=1), preferred_element_type=jnp.float32
        )
        slope_ref[p] = slopes.astype(jnp.bfloat16)
        for c in range(COMPS):
            row_ref[p, c * 8 : (c + 1) * 8] = slopes[c * wide + main : c * wide + main + 8]

    def repeated(row):
        return jnp.broadcast_to(row, (PACK, LANES)).astype(jnp.bfloat16)

    def along(left, right):
        term = left[0] * right[0]
        for d in range(1, COMPS):
            term = term + left[d] * right[d]
        return term

    def fill(prod_ref, p, v):
        here = slice(v * LANES, (v + 1) * LANES)

        def there(d):
            return slice((d * inner + v) * LANES, (d * inner + v + 1) * LANES)

        def lanes(c):
            return slice((v * COMPS + c) * LANES, (v * COMPS + c + 1) * LANES)

        slopes = {
            (c, j): [slope_ref[p, c * wide + j : c * wide + j + PACK, there(d)] for d in range(COMPS)]
            for c in range(COMPS)
            for j in range(0, main, PACK)
        }
        for i in range(plan.modes):
            moving = [repeated(moving_ref[p, d * wide + i : d * wide + i + 1, here]) for d in range(COMPS)]
            for c in range(COMPS):
                for j in range(0, main, PACK):
                    prod_ref[i * main + j : i * main + j + PACK, lanes(c)] = along(moving, slopes[c, j])
        if plan.rest:
            moving = {
                i: [moving_ref[p, d * wide + i : d * wide + i + PACK, here].astype(jnp.bfloat16) for d in range(COMPS)]
                for i in range(0, wide, PACK)
            }
            for c in range(COMPS):
                for j in range(plan.rest):
                    slope = [repeated(row_ref[p, c * 8 + j : c * 8 + j + 1, there(d)]) for d in range(COMPS)]
                    for i in range(0, wide, PACK):
                        at = plan.pairs + j * wide + i
                        prod_ref[at : at + PACK, lanes(c)] = along(moving[i], slope)

    def multiply(slot, prod_ref, cut):
        low, high = cut
        result = jnp.dot(table_ref[...], prod_ref[:, low:high], preferred_element_type=jnp.float32)
        for at in range(low, high, LANES):
            v, c = divmod(at // LANES, COMPS)
            conv_ref[slot, v, c * pad : (c + 1) * pad, :] = result[:, at - low : at - low + LANES]

    def beside(prod_ref, p, done_ref, slot):
        cuts = list(plan.cuts)
        for v in range(inner):
            if cuts:
                multiply(slot, done_ref, cuts.pop(0))
            fill(prod_ref, p, v)
        for cut in cuts:
            multiply(slot, done_ref, cut)

    def two_planes(step, carry):
        p = 2 * step
        beside(even_ref, p, odd_ref, p)
        beside(odd_ref, p + 1, even_ref, p + 1)
        return carry

    lax.fori_loop(0, planes // 2, two_planes, 0)
    for cut in plan.cuts:
        multiply(planes, odd_ref, cut)
    for p in range(planes):
        stacked = jnp.concatenate([conv_ref[p + 1, v].astype(jnp.bfloat16) for v in range(inner)], axis=1)
        placed = jnp.dot(place_ref[...], stacked, preferred_element_type=jnp.float32).astype(jnp.bfloat16)
        for v in range(inner):
            block = placed[:, v * LANES : (v + 1) * LANES]
            out_ref[p, :, v] = block.reshape(plan.chunks, plan.packed, LANES)


def finish_kernel(plan, got_ref, base_ref, swap_ref, conv_ref, next_ref, flat_ref, conv_vmem, next_vmem, sems):
    for v in range(plan.inner):
        parts = [got_ref[s, :, v].reshape(plan.wide, LANES) for s in range(plan.planes)]
        swapped = jnp.dot(jnp.concatenate(parts, axis=1), swap_ref[...], preferred_element_type=jnp.float32)
        for block in range(min(plan.planes, plan.rows - v * plan.planes)):
            for chunk in range(plan.chunks):
                at = (chunk * plan.rows + v * plan.planes + block) * plan.packed
                flat_ref[at : at + plan.packed, :] = swapped[
                    chunk * plan.packed : (chunk + 1) * plan.packed, block * LANES : (block + 1) * LANES
                ]
    copies = []
    for s in range(plan.slot_dev):
        fields = slice(s * COMPS, (s + 1) * COMPS)
        for f in range(s * COMPS, (s + 1) * COMPS):
            value = flat_ref[pl.ds(f, plan.ny, stride=plan.packed), :]
            conv_vmem[f] = value
            next_vmem[f] = base_ref[f] - SECTION_STEP * value
        for which, (source, target) in enumerate(((conv_vmem, conv_ref), (next_vmem, next_ref))):
            copies.append(pltpu.make_async_copy(source.at[fields], target.at[fields], sems.at[which, s]))
            copies[-1].start()
    for copy in copies:
        copy.wait()


def on_device(velocity, base_velocity, mode_slot, triples, triple_coef):
    slot_dev, _, _, ny, nz = velocity.shape
    chunks, planes = lax.axis_size("chaos"), lax.axis_size("space")
    plan = Plan(slot_dev, ny, nz, planes, chunks, mode_slot.shape[0])
    fields, packed, devices = plan.fields, plan.packed, planes * chunks

    def exchange(block):
        flat = block.reshape((devices,) + block.shape[2:])
        return lax.all_to_all(flat, ("space", "chaos"), 0, 0, tiled=True).reshape(block.shape)

    sent = pl.pallas_call(
        functools.partial(pack_kernel, plan),
        out_shape=jax.ShapeDtypeStruct((planes, chunks, plan.vectors, packed, LANES), jnp.bfloat16),
        in_specs=[vmem_spec()],
        out_specs=vmem_spec(),
        compiler_params=params(),
        name="pack",
    )(velocity.reshape(fields * ny, nz))
    got = exchange(sent)
    table, pick, place, swap = pl.pallas_call(
        functools.partial(prepare_kernel, plan),
        out_shape=[
            jax.ShapeDtypeStruct((plan.mode_pad, plan.depth), jnp.bfloat16),
            jax.ShapeDtypeStruct((COMPS * plan.wide_pad, plan.wide), jnp.bfloat16),
            jax.ShapeDtypeStruct((plan.wide, COMPS * plan.mode_pad), jnp.bfloat16),
            jax.ShapeDtypeStruct((planes * LANES, planes * LANES), jnp.bfloat16),
        ],
        in_specs=[pl.BlockSpec(memory_space=pltpu.SMEM)] + [vmem_spec()] * 2,
        out_specs=[vmem_spec()] * 4,
        compiler_params=params(),
        name="prepare",
    )(mode_slot, triples.T, triple_coef.reshape(1, -1))
    returned = pl.pallas_call(
        functools.partial(contract_kernel, plan),
        out_shape=jax.ShapeDtypeStruct((planes, chunks, plan.inner, packed, LANES), jnp.bfloat16),
        in_specs=[vmem_spec()] * 5,
        out_specs=vmem_spec(),
        scratch_shapes=[
            pltpu.VMEM((planes, COMPS * plan.wide_pad, plan.inner * LANES), jnp.float32),
            pltpu.VMEM((planes, COMPS * 8, plan.lanes), jnp.float32),
            pltpu.VMEM((planes, COMPS * plan.wide_pad, plan.lanes), jnp.bfloat16),
            pltpu.VMEM((planes + 1, plan.inner, COMPS * plan.mode_pad, LANES), jnp.float32),
            pltpu.VMEM((plan.depth, plan.lanes), jnp.bfloat16),
            pltpu.VMEM((plan.depth, plan.lanes), jnp.bfloat16),
        ],
        compiler_params=params(),
        name="contract",
    )(got, jnp.asarray(plan.stencil(), jnp.bfloat16), table, pick, place)
    convection, next_velocity = pl.pallas_call(
        functools.partial(finish_kernel, plan),
        out_shape=[jax.ShapeDtypeStruct((fields, ny, nz), jnp.float32)] * 2,
        in_specs=[vmem_spec()] * 3,
        out_specs=[pl.BlockSpec(memory_space=pl.ANY)] * 2,
        scratch_shapes=[
            pltpu.VMEM((ny * packed, LANES), jnp.float32),
            pltpu.VMEM((fields, ny, nz), jnp.float32),
            pltpu.VMEM((fields, ny, nz), jnp.float32),
            pltpu.SemaphoreType.DMA((2, slot_dev)),
        ],
        compiler_params=params(),
        name="finish",
    )(exchange(returned), base_velocity.reshape(fields, ny, nz), swap)
    return convection.reshape(velocity.shape), next_velocity.reshape(velocity.shape)


def solution(mesh):
    spread = P("chaos", None, "space", None, None)
    return jax.shard_map(
        on_device,
        mesh=mesh,
        in_specs=(spread, spread, P(), P(), P()),
        out_specs=(spread, spread),
        check_vma=False,
    )
```

```python
import functools

import jax
import jax.numpy as jnp
import numpy as np
from jax import lax
from jax.experimental import pallas as pl
from jax.experimental.pallas import tpu as pltpu
from jax.sharding import PartitionSpec as P

SECTION_STEP = 0.5
COMPS = 3
LANES = 128
LANE_BITS = 7
TILE = 256
PACK = 16
VMEM_LIMIT = 48 * 1024 * 1024


def round_up(value, unit):
    return -(-value // unit) * unit


def vmem_spec():
    return pl.BlockSpec(memory_space=pltpu.VMEM)


def params():
    return pltpu.CompilerParams(vmem_limit_bytes=VMEM_LIMIT)


class Plan:
    def __init__(self, slot_dev, ny, nz, planes, chunks, modes):
        self.slot_dev, self.ny, self.planes, self.chunks, self.modes = slot_dev, ny, planes, chunks, modes
        self.fields = slot_dev * COMPS
        self.packed = round_up(self.fields, 16)
        self.wide = chunks * self.packed
        self.rows = ny // chunks
        self.width = nz // planes
        assert nz == LANES and self.width * planes == nz and self.rows * chunks == ny
        self.width_bits = self.width.bit_length() - 1
        assert self.rest_fits(modes)
        assert planes & (planes - 1) == 0 and 2 * self.rows <= self.width
        self.inner = -(-self.rows // planes)
        if self.rows % planes == 0:
            assert planes >= 3
            self.vectors = self.inner + 1
            first = self.inner * planes
            self.low, self.high, self.side = first, first + 1, first + 2
        else:
            assert self.rows + 3 <= planes
            self.vectors = 1
            self.low, self.high, self.side = planes - 1, self.rows, self.rows + 1
        self.mode_pad = round_up(modes, 8)
        self.main = modes // 16 * 16
        self.rest = modes - self.main
        self.wide_pad = round_up(modes, PACK)
        self.rest_rows = self.rest * self.wide_pad
        self.pairs = modes * self.main
        self.depth = round_up(self.pairs + self.rest_rows, TILE)
        self.groups = self.depth // TILE
        self.lanes = self.inner * COMPS * LANES
        self.cuts = [(at, min(at + TILE, self.lanes)) for at in range(0, self.lanes, TILE)]

    @staticmethod
    def rest_fits(modes):
        return modes >= PACK and modes % PACK <= 8

    def stencil(self):
        out = np.zeros((self.vectors * LANES, 2 * self.inner * LANES), np.float32)
        width = self.width
        for r in range(self.rows):
            above = r + 1 if r + 1 < self.rows else self.high
            below = r - 1 if r > 0 else self.low
            for w in range(width):
                at = r * width + w
                out[above * width + w, at] += 0.5
                out[below * width + w, at] -= 0.5
                right = at + 1 if w + 1 < width else self.side * width + 2 * r + 1
                left = at - 1 if w > 0 else self.side * width + 2 * r
                out[right, self.inner * LANES + at] += 0.5
                out[left, self.inner * LANES + at] -= 0.5
        return out


def block_transposer(plan):
    shape = (plan.planes * LANES, LANES)
    source = lax.broadcasted_iota(jnp.int32, shape, 0)
    target = lax.broadcasted_iota(jnp.int32, shape, 1)
    part, lane = source >> LANE_BITS, source & (LANES - 1)
    block, inner = lane >> plan.width_bits, lane & (plan.width - 1)
    wanted = (block << LANE_BITS) + (part << plan.width_bits) + inner
    return jnp.concatenate(
        [jnp.where(wanted == target + b * LANES, 1.0, 0.0).astype(jnp.bfloat16) for b in range(plan.planes)], axis=1
    )


def side_collector(plan):
    source = lax.broadcasted_iota(jnp.int32, (plan.rows * LANES, LANES), 0)
    target = lax.broadcasted_iota(jnp.int32, (1, LANES), 1)
    block, inner = target >> plan.width_bits, target & (plan.width - 1)
    beside = (block << plan.width_bits) - 1 + (inner & 1) * (plan.width + 1)
    wanted = ((inner >> 1) << LANE_BITS) + (beside & (LANES - 1))
    wanted = jnp.where(inner < 2 * plan.rows, wanted, -1)
    return jnp.where(source == wanted, 1.0, 0.0).astype(jnp.bfloat16)


def pack_kernel(plan, v_hbm, out_hbm, v_ref, out_ref, in_sem, out_sems):
    planes, rows, chunks, packed = plan.planes, plan.rows, plan.chunks, plan.packed
    fetch = pltpu.make_async_copy(v_hbm, v_ref, in_sem)
    fetch.start()
    transposer = block_transposer(plan)
    collector = side_collector(plan)
    fetch.wait()
    pad = jnp.zeros((packed - plan.fields, LANES), jnp.float32)
    lines = []
    for y in range(plan.ny):
        block = v_ref[pl.ds(y, plan.fields, stride=plan.ny), :]
        lines.append(jnp.concatenate([block, pad], axis=0).astype(jnp.bfloat16))

    def across(offset):
        return jnp.concatenate([lines[(c * rows + offset) % plan.ny] for c in range(chunks)], axis=0)

    inside = [across(r) for r in range(rows)]
    side = jnp.dot(jnp.concatenate(inside, axis=1), collector, preferred_element_type=jnp.float32)
    blocks = inside + [jnp.zeros_like(inside[0])] * (plan.vectors * planes - rows)
    blocks[plan.low] = across(-1)
    blocks[plan.high] = across(rows)
    blocks[plan.side] = side.astype(jnp.bfloat16)
    copies = []
    for v in range(plan.vectors):
        row = jnp.concatenate(blocks[v * planes : (v + 1) * planes], axis=1)
        swapped = jnp.dot(row, transposer, preferred_element_type=jnp.float32).astype(jnp.bfloat16)
        for s in range(planes):
            for c in range(chunks):
                out_ref[s, c, v] = swapped[c * packed : (c + 1) * packed, s * LANES : (s + 1) * LANES]
        copies.append(pltpu.make_async_copy(out_ref.at[:, :, v], out_hbm.at[:, :, v], out_sems.at[v]))
        copies[-1].start()
    for copy in copies:
        copy.wait()


def prepare_kernel(plan, slot_ref, triples_ref, coef_ref, table_ref, pick_ref, place_ref, swap_ref):
    count = triples_ref.shape[1]
    mode_i = triples_ref[0:1, :]
    mode_j = triples_ref[1:2, :]
    mode_k = triples_ref[2:3, :]
    place = jnp.where(
        mode_j < plan.main,
        mode_i * plan.main + mode_j,
        plan.pairs + (mode_j - plan.main) * plan.wide_pad + mode_i,
    )
    row = (place // TILE) * plan.mode_pad + mode_k
    column = place % TILE
    coef = coef_ref[...].astype(jnp.float32)
    height = plan.groups * plan.mode_pad
    total = jnp.zeros((height, TILE), jnp.float32)
    step = 1024 if count % 1024 == 0 else count
    row_iota = lax.broadcasted_iota(jnp.int32, (height, step), 0)
    column_iota = lax.broadcasted_iota(jnp.int32, (TILE, step), 0)
    for start in range(0, count, step):
        part = slice(start, start + step)
        left = jnp.where(row_iota == row[:, part], coef[:, part], 0.0).astype(jnp.bfloat16)
        right = jnp.where(column_iota == column[:, part], 1.0, 0.0).astype(jnp.bfloat16)
        total = total + lax.dot_general(
            left, right, (((1,), (1,)), ((), ())), preferred_element_type=jnp.float32
        )
    for g in range(plan.groups):
        table_ref[:, g * TILE : (g + 1) * TILE] = total[g * plan.mode_pad : (g + 1) * plan.mode_pad].astype(jnp.bfloat16)

    shape = (plan.wide_pad, plan.wide)
    column = lax.broadcasted_iota(jnp.int32, shape, 1)
    mode = lax.broadcasted_iota(jnp.int32, shape, 0)
    inner = column % plan.packed
    slot = jnp.where(
        inner < plan.fields, (column // plan.packed) * plan.slot_dev + inner // COMPS, -1
    )
    wanted = jnp.full(shape, -2, jnp.int32)
    for m in range(plan.modes):
        wanted = jnp.where(mode == m, slot_ref[m], wanted)
    hit = jnp.where(wanted == slot, 1.0, 0.0)
    pickers = [jnp.where(inner % COMPS == d, hit, 0.0) for d in range(COMPS)]
    pick_ref[...] = jnp.concatenate(pickers, axis=0).astype(jnp.bfloat16)
    narrow = jnp.concatenate([picker[: plan.mode_pad] for picker in pickers], axis=0)
    place_ref[...] = narrow.T.astype(jnp.bfloat16)
    swap_ref[...] = block_transposer(plan)


def contract_kernel(plan, got_ref, stencil_ref, table_ref, pick_ref, place_ref, out_ref, *scratch):
    conv_ref, even_ref, odd_ref = scratch[:3]
    even_fields, odd_fields = scratch[3:6], scratch[6:9]
    planes, inner, pad, main, wide = plan.planes, plan.inner, plan.mode_pad, plan.main, plan.wide_pad
    tail = plan.pairs + plan.rest_rows
    if tail < plan.depth:
        for ref in (even_ref, odd_ref):
            ref[tail:, :] = jnp.zeros((plan.depth - tail, ref.shape[1]), jnp.bfloat16)

    def vector(p, v):
        return got_ref[lax.rem(p, planes), :, v].reshape(plan.wide, LANES)

    def prepare(fields, p):
        moving_ref, row_ref, slope_ref = fields
        center = jnp.concatenate([vector(p, v) for v in range(plan.vectors)], axis=1)
        along_x = []
        for v in range(inner):
            ahead, behind = vector(p + 1, v), vector(p + planes - 1, v)
            along_x.append((0.5 * (ahead.astype(jnp.float32) - behind.astype(jnp.float32))).astype(jnp.bfloat16))
        along_yz = jnp.dot(center, stencil_ref[...], preferred_element_type=jnp.float32).astype(jnp.bfloat16)
        moving = center[:, : inner * LANES]
        moving_ref[...] = jnp.dot(pick_ref[...], moving, preferred_element_type=jnp.float32)
        slopes = jnp.dot(
            pick_ref[...], jnp.concatenate(along_x + [along_yz], axis=1), preferred_element_type=jnp.float32
        )
        slope_ref[...] = slopes.astype(jnp.bfloat16)
        for c in range(COMPS):
            row_ref[c * 8 : (c + 1) * 8] = slopes[c * wide + main : c * wide + main + 8]

    def repeated(row):
        return jnp.broadcast_to(row, (PACK, LANES)).astype(jnp.bfloat16)

    def along(left, right):
        term = left[0] * right[0]
        for d in range(1, COMPS):
            term = term + left[d] * right[d]
        return term

    def fill(prod_ref, fields, v):
        moving_ref, row_ref, slope_ref = fields
        here = slice(v * LANES, (v + 1) * LANES)

        def there(d):
            return slice((d * inner + v) * LANES, (d * inner + v + 1) * LANES)

        def lanes(c):
            return slice((v * COMPS + c) * LANES, (v * COMPS + c + 1) * LANES)

        slopes = {
            (c, j): [slope_ref[c * wide + j : c * wide + j + PACK, there(d)] for d in range(COMPS)]
            for c in range(COMPS)
            for j in range(0, main, PACK)
        }
        for i in range(plan.modes):
            moving = [repeated(moving_ref[d * wide + i : d * wide + i + 1, here]) for d in range(COMPS)]
            for c in range(COMPS):
                for j in range(0, main, PACK):
                    prod_ref[i * main + j : i * main + j + PACK, lanes(c)] = along(moving, slopes[c, j])
        if plan.rest:
            moving = {
                i: [moving_ref[d * wide + i : d * wide + i + PACK, here].astype(jnp.bfloat16) for d in range(COMPS)]
                for i in range(0, wide, PACK)
            }
            for c in range(COMPS):
                for j in range(plan.rest):
                    slope = [repeated(row_ref[c * 8 + j : c * 8 + j + 1, there(d)]) for d in range(COMPS)]
                    for i in range(0, wide, PACK):
                        at = plan.pairs + j * wide + i
                        prod_ref[at : at + PACK, lanes(c)] = along(moving[i], slope)

    def multiply(slot, prod_ref, cut):
        low, high = cut
        result = jnp.dot(table_ref[...], prod_ref[:, low:high], preferred_element_type=jnp.float32)
        for at in range(low, high, LANES):
            v, c = divmod(at // LANES, COMPS)
            conv_ref[slot, v, c * pad : (c + 1) * pad, :] = result[:, at - low : at - low + LANES]

    def beside(prod_ref, fields, done_ref, slot):
        cuts = list(plan.cuts)
        for v in range(inner):
            if cuts:
                multiply(slot, done_ref, cuts.pop(0))
            fill(prod_ref, fields, v)
        for cut in cuts:
            multiply(slot, done_ref, cut)

    def two_planes(step, carry):
        p = 2 * step
        prepare(odd_fields, p + 1)
        beside(even_ref, even_fields, odd_ref, p)
        prepare(even_fields, p + 2)
        beside(odd_ref, odd_fields, even_ref, p + 1)
        return carry

    prepare(even_fields, 0)
    lax.fori_loop(0, planes // 2, two_planes, 0)
    for cut in plan.cuts:
        multiply(planes, odd_ref, cut)
    for p in range(planes):
        stacked = jnp.concatenate([conv_ref[p + 1, v].astype(jnp.bfloat16) for v in range(inner)], axis=1)
        placed = jnp.dot(place_ref[...], stacked, preferred_element_type=jnp.float32).astype(jnp.bfloat16)
        for v in range(inner):
            block = placed[:, v * LANES : (v + 1) * LANES]
            out_ref[p, :, v] = block.reshape(plan.chunks, plan.packed, LANES)


def finish_kernel(plan, got_ref, base_ref, swap_ref, conv_ref, next_ref, flat_ref, conv_vmem, next_vmem, sems):
    for v in range(plan.inner):
        parts = [got_ref[s, :, v].reshape(plan.wide, LANES) for s in range(plan.planes)]
        swapped = jnp.dot(jnp.concatenate(parts, axis=1), swap_ref[...], preferred_element_type=jnp.float32)
        for block in range(min(plan.planes, plan.rows - v * plan.planes)):
            for chunk in range(plan.chunks):
                at = (chunk * plan.rows + v * plan.planes + block) * plan.packed
                flat_ref[at : at + plan.packed, :] = swapped[
                    chunk * plan.packed : (chunk + 1) * plan.packed, block * LANES : (block + 1) * LANES
                ]
    copies = []
    for s in range(plan.slot_dev):
        fields = slice(s * COMPS, (s + 1) * COMPS)
        for f in range(s * COMPS, (s + 1) * COMPS):
            value = flat_ref[pl.ds(f, plan.ny, stride=plan.packed), :]
            conv_vmem[f] = value
            next_vmem[f] = base_ref[f] - SECTION_STEP * value
        for which, (source, target) in enumerate(((conv_vmem, conv_ref), (next_vmem, next_ref))):
            copies.append(pltpu.make_async_copy(source.at[fields], target.at[fields], sems.at[which, s]))
            copies[-1].start()
    for copy in copies:
        copy.wait()


def on_device(velocity, base_velocity, mode_slot, triples, triple_coef):
    slot_dev, _, _, ny, nz = velocity.shape
    chunks, planes = lax.axis_size("chaos"), lax.axis_size("space")
    plan = Plan(slot_dev, ny, nz, planes, chunks, mode_slot.shape[0])
    fields, packed, devices = plan.fields, plan.packed, planes * chunks

    def exchange(block):
        flat = block.reshape((devices,) + block.shape[2:])
        return lax.all_to_all(flat, ("space", "chaos"), 0, 0, tiled=True).reshape(block.shape)

    sent = pl.pallas_call(
        functools.partial(pack_kernel, plan),
        out_shape=jax.ShapeDtypeStruct((planes, chunks, plan.vectors, packed, LANES), jnp.bfloat16),
        in_specs=[pl.BlockSpec(memory_space=pl.ANY)],
        out_specs=pl.BlockSpec(memory_space=pl.ANY),
        scratch_shapes=[
            pltpu.VMEM((fields * ny, nz), jnp.float32),
            pltpu.VMEM((planes, chunks, plan.vectors, packed, LANES), jnp.bfloat16),
            pltpu.SemaphoreType.DMA,
            pltpu.SemaphoreType.DMA((plan.vectors,)),
        ],
        compiler_params=params(),
        name="pack",
    )(velocity.reshape(fields * ny, nz))
    got = exchange(sent)
    table, pick, place, swap = pl.pallas_call(
        functools.partial(prepare_kernel, plan),
        out_shape=[
            jax.ShapeDtypeStruct((plan.mode_pad, plan.depth), jnp.bfloat16),
            jax.ShapeDtypeStruct((COMPS * plan.wide_pad, plan.wide), jnp.bfloat16),
            jax.ShapeDtypeStruct((plan.wide, COMPS * plan.mode_pad), jnp.bfloat16),
            jax.ShapeDtypeStruct((planes * LANES, planes * LANES), jnp.bfloat16),
        ],
        in_specs=[pl.BlockSpec(memory_space=pltpu.SMEM)] + [vmem_spec()] * 2,
        out_specs=[vmem_spec()] * 4,
        compiler_params=params(),
        name="prepare",
    )(mode_slot, triples.T, triple_coef.reshape(1, -1))
    returned = pl.pallas_call(
        functools.partial(contract_kernel, plan),
        out_shape=jax.ShapeDtypeStruct((planes, chunks, plan.inner, packed, LANES), jnp.bfloat16),
        in_specs=[vmem_spec()] * 5,
        out_specs=vmem_spec(),
        scratch_shapes=[
            pltpu.VMEM((planes + 1, plan.inner, COMPS * plan.mode_pad, LANES), jnp.float32),
            pltpu.VMEM((plan.depth, plan.lanes), jnp.bfloat16),
            pltpu.VMEM((plan.depth, plan.lanes), jnp.bfloat16),
        ]
        + [
            pltpu.VMEM((COMPS * plan.wide_pad, plan.inner * LANES), jnp.float32),
            pltpu.VMEM((COMPS * 8, plan.lanes), jnp.float32),
            pltpu.VMEM((COMPS * plan.wide_pad, plan.lanes), jnp.bfloat16),
        ]
        * 2,
        compiler_params=params(),
        name="contract",
    )(got, jnp.asarray(plan.stencil(), jnp.bfloat16), table, pick, place)
    convection, next_velocity = pl.pallas_call(
        functools.partial(finish_kernel, plan),
        out_shape=[jax.ShapeDtypeStruct((fields, ny, nz), jnp.float32)] * 2,
        in_specs=[vmem_spec()] * 3,
        out_specs=[pl.BlockSpec(memory_space=pl.ANY)] * 2,
        scratch_shapes=[
            pltpu.VMEM((ny * packed, LANES), jnp.float32),
            pltpu.VMEM((fields, ny, nz), jnp.float32),
            pltpu.VMEM((fields, ny, nz), jnp.float32),
            pltpu.SemaphoreType.DMA((2, slot_dev)),
        ],
        compiler_params=params(),
        name="finish",
    )(exchange(returned), base_velocity.reshape(fields, ny, nz), swap)
    return convection.reshape(velocity.shape), next_velocity.reshape(velocity.shape)


def solution(mesh):
    spread = P("chaos", None, "space", None, None)
    return jax.shard_map(
        on_device,
        mesh=mesh,
        in_specs=(spread, spread, P(), P(), P()),
        out_specs=(spread, spread),
        check_vma=False,
    )
```

```python
import functools

import jax
import jax.numpy as jnp
import numpy as np
from jax import lax
from jax.experimental import pallas as pl
from jax.experimental.pallas import tpu as pltpu
from jax.sharding import PartitionSpec as P

SECTION_STEP = 0.5
COMPS = 3
LANES = 128
LANE_BITS = 7
TILE = 256
PACK = 16
VMEM_LIMIT = 48 * 1024 * 1024
PACK_VMEM_LIMIT = 65280 * 1024


def round_up(value, unit):
    return -(-value // unit) * unit


def vmem_spec():
    return pl.BlockSpec(memory_space=pltpu.VMEM)


def params(limit=VMEM_LIMIT):
    return pltpu.CompilerParams(vmem_limit_bytes=limit)


class Plan:
    def __init__(self, slot_dev, ny, nz, planes, chunks, modes):
        self.slot_dev, self.ny, self.planes, self.chunks, self.modes = slot_dev, ny, planes, chunks, modes
        self.fields = slot_dev * COMPS
        self.packed = round_up(self.fields, 16)
        self.wide = chunks * self.packed
        self.rows = ny // chunks
        self.width = nz // planes
        assert nz == LANES and self.width * planes == nz and self.rows * chunks == ny
        self.width_bits = self.width.bit_length() - 1
        assert self.rest_fits(modes)
        assert planes & (planes - 1) == 0 and 2 * self.rows <= self.width
        self.inner = -(-self.rows // planes)
        if self.rows % planes == 0:
            assert planes >= 3
            self.vectors = self.inner + 1
            first = self.inner * planes
            self.low, self.high, self.side = first, first + 1, first + 2
        else:
            assert self.rows + 3 <= planes
            self.vectors = 1
            self.low, self.high, self.side = planes - 1, self.rows, self.rows + 1
        self.mode_pad = round_up(modes, 8)
        self.main = modes // 16 * 16
        self.rest = modes - self.main
        self.wide_pad = round_up(modes, PACK)
        self.rest_rows = self.rest * self.wide_pad
        self.pairs = modes * self.main
        self.depth = round_up(self.pairs + self.rest_rows, TILE)
        self.groups = self.depth // TILE
        self.lanes = self.inner * COMPS * LANES
        self.cuts = [(at, min(at + TILE, self.lanes)) for at in range(0, self.lanes, TILE)]

    @staticmethod
    def rest_fits(modes):
        return modes >= PACK and modes % PACK <= 8

    def stencil(self):
        out = np.zeros((self.vectors * LANES, 2 * self.inner * LANES), np.float32)
        width = self.width
        for r in range(self.rows):
            above = r + 1 if r + 1 < self.rows else self.high
            below = r - 1 if r > 0 else self.low
            for w in range(width):
                at = r * width + w
                out[above * width + w, at] += 0.5
                out[below * width + w, at] -= 0.5
                right = at + 1 if w + 1 < width else self.side * width + 2 * r + 1
                left = at - 1 if w > 0 else self.side * width + 2 * r
                out[right, self.inner * LANES + at] += 0.5
                out[left, self.inner * LANES + at] -= 0.5
        return out


def block_transposer(plan):
    shape = (plan.planes * LANES, LANES)
    source = lax.broadcasted_iota(jnp.int32, shape, 0)
    target = lax.broadcasted_iota(jnp.int32, shape, 1)
    part, lane = source >> LANE_BITS, source & (LANES - 1)
    block, inner = lane >> plan.width_bits, lane & (plan.width - 1)
    wanted = (block << LANE_BITS) + (part << plan.width_bits) + inner
    return jnp.concatenate(
        [jnp.where(wanted == target + b * LANES, 1.0, 0.0).astype(jnp.bfloat16) for b in range(plan.planes)], axis=1
    )


def side_collector(plan):
    source = lax.broadcasted_iota(jnp.int32, (plan.rows * LANES, LANES), 0)
    target = lax.broadcasted_iota(jnp.int32, (1, LANES), 1)
    block, inner = target >> plan.width_bits, target & (plan.width - 1)
    beside = (block << plan.width_bits) - 1 + (inner & 1) * (plan.width + 1)
    wanted = ((inner >> 1) << LANE_BITS) + (beside & (LANES - 1))
    wanted = jnp.where(inner < 2 * plan.rows, wanted, -1)
    return jnp.where(source == wanted, 1.0, 0.0).astype(jnp.bfloat16)


def pack_kernel(plan, v_hbm, out_hbm, v_ref, out_ref, in_sem, out_sems):
    planes, rows, chunks, packed = plan.planes, plan.rows, plan.chunks, plan.packed
    fetch = pltpu.make_async_copy(v_hbm, v_ref, in_sem)
    fetch.start()
    transposer = block_transposer(plan)
    collector = side_collector(plan)
    fetch.wait()
    pad = jnp.zeros((packed - plan.fields, LANES), jnp.float32)
    lines = []
    for y in range(plan.ny):
        block = v_ref[pl.ds(y, plan.fields, stride=plan.ny), :]
        lines.append(jnp.concatenate([block, pad], axis=0).astype(jnp.bfloat16))

    def across(offset):
        return jnp.concatenate([lines[(c * rows + offset) % plan.ny] for c in range(chunks)], axis=0)

    inside = [across(r) for r in range(rows)]
    side = jnp.dot(jnp.concatenate(inside, axis=1), collector, preferred_element_type=jnp.float32)
    blocks = inside + [jnp.zeros_like(inside[0])] * (plan.vectors * planes - rows)
    blocks[plan.low] = across(-1)
    blocks[plan.high] = across(rows)
    blocks[plan.side] = side.astype(jnp.bfloat16)
    copies = []
    for v in range(plan.vectors):
        row = jnp.concatenate(blocks[v * planes : (v + 1) * planes], axis=1)
        swapped = jnp.dot(row, transposer, preferred_element_type=jnp.float32).astype(jnp.bfloat16)
        for s in range(planes):
            for c in range(chunks):
                out_ref[s, c, v] = swapped[c * packed : (c + 1) * packed, s * LANES : (s + 1) * LANES]
        copies.append(pltpu.make_async_copy(out_ref.at[:, :, v], out_hbm.at[:, :, v], out_sems.at[v]))
        copies[-1].start()
    for copy in copies:
        copy.wait()


def prepare_kernel(plan, slot_ref, triples_ref, coef_ref, table_ref, pick_ref, place_ref, swap_ref):
    count = triples_ref.shape[1]
    mode_i = triples_ref[0:1, :]
    mode_j = triples_ref[1:2, :]
    mode_k = triples_ref[2:3, :]
    place = jnp.where(
        mode_j < plan.main,
        mode_i * plan.main + mode_j,
        plan.pairs + (mode_j - plan.main) * plan.wide_pad + mode_i,
    )
    row = (place // TILE) * plan.mode_pad + mode_k
    column = place % TILE
    coef = coef_ref[...].astype(jnp.float32)
    height = plan.groups * plan.mode_pad
    total = jnp.zeros((height, TILE), jnp.float32)
    step = 1024 if count % 1024 == 0 else count
    row_iota = lax.broadcasted_iota(jnp.int32, (height, step), 0)
    column_iota = lax.broadcasted_iota(jnp.int32, (TILE, step), 0)
    for start in range(0, count, step):
        part = slice(start, start + step)
        left = jnp.where(row_iota == row[:, part], coef[:, part], 0.0).astype(jnp.bfloat16)
        right = jnp.where(column_iota == column[:, part], 1.0, 0.0).astype(jnp.bfloat16)
        total = total + lax.dot_general(
            left, right, (((1,), (1,)), ((), ())), preferred_element_type=jnp.float32
        )
    for g in range(plan.groups):
        table_ref[:, g * TILE : (g + 1) * TILE] = total[g * plan.mode_pad : (g + 1) * plan.mode_pad].astype(jnp.bfloat16)

    shape = (plan.wide_pad, plan.wide)
    column = lax.broadcasted_iota(jnp.int32, shape, 1)
    mode = lax.broadcasted_iota(jnp.int32, shape, 0)
    inner = column % plan.packed
    slot = jnp.where(
        inner < plan.fields, (column // plan.packed) * plan.slot_dev + inner // COMPS, -1
    )
    wanted = jnp.full(shape, -2, jnp.int32)
    for m in range(plan.modes):
        wanted = jnp.where(mode == m, slot_ref[m], wanted)
    hit = jnp.where(wanted == slot, 1.0, 0.0)
    pickers = [jnp.where(inner % COMPS == d, hit, 0.0) for d in range(COMPS)]
    pick_ref[...] = jnp.concatenate(pickers, axis=0).astype(jnp.bfloat16)
    narrow = jnp.concatenate([picker[: plan.mode_pad] for picker in pickers], axis=0)
    place_ref[...] = narrow.T.astype(jnp.bfloat16)
    swap_ref[...] = block_transposer(plan)


def contract_kernel(plan, got_ref, stencil_ref, table_ref, pick_ref, place_ref, out_ref, *scratch):
    conv_ref, beside_ref = scratch[:2]
    prod_refs, field_refs = scratch[2:4], (scratch[4:7], scratch[7:10])
    planes, inner, pad, main, wide = plan.planes, plan.inner, plan.mode_pad, plan.main, plan.wide_pad
    tail = plan.pairs + plan.rest_rows
    if tail < plan.depth:
        for ref in prod_refs:
            ref[tail:, :] = jnp.zeros((plan.depth - tail, ref.shape[1]), jnp.bfloat16)

    def vector(p, v):
        return got_ref[p % planes, :, v].reshape(plan.wide, LANES)

    centers = [jnp.concatenate([vector(p, v) for v in range(plan.vectors)], axis=1) for p in range(planes)]
    beside_ref[...] = jnp.dot(
        jnp.concatenate(centers, axis=0), stencil_ref[...], preferred_element_type=jnp.float32
    ).astype(jnp.bfloat16)

    def prepare(fields, p):
        moving_ref, row_ref, slope_ref = fields
        parts = [vector(p, v) for v in range(inner)]
        for v in range(inner):
            ahead, behind = vector(p + 1, v), vector(p - 1, v)
            parts.append((0.5 * (ahead.astype(jnp.float32) - behind.astype(jnp.float32))).astype(jnp.bfloat16))
        parts.append(beside_ref[p * plan.wide : (p + 1) * plan.wide, :])
        picked = jnp.dot(pick_ref[...], jnp.concatenate(parts, axis=1), preferred_element_type=jnp.float32)
        moving_ref[...] = picked[:, : inner * LANES]
        slopes = picked[:, inner * LANES :]
        slope_ref[...] = slopes.astype(jnp.bfloat16)
        for c in range(COMPS):
            row_ref[c * 8 : (c + 1) * 8] = slopes[c * wide + main : c * wide + main + 8]

    def repeated(row):
        return jnp.broadcast_to(row, (PACK, LANES)).astype(jnp.bfloat16)

    def along(left, right):
        term = left[0] * right[0]
        for d in range(1, COMPS):
            term = term + left[d] * right[d]
        return term

    def fill(prod_ref, fields, v):
        moving_ref, row_ref, slope_ref = fields
        here = slice(v * LANES, (v + 1) * LANES)

        def there(d):
            return slice((d * inner + v) * LANES, (d * inner + v + 1) * LANES)

        def lanes(c):
            return slice((v * COMPS + c) * LANES, (v * COMPS + c + 1) * LANES)

        slopes = {
            (c, j): [slope_ref[c * wide + j : c * wide + j + PACK, there(d)] for d in range(COMPS)]
            for c in range(COMPS)
            for j in range(0, main, PACK)
        }
        for i in range(plan.modes):
            moving = [repeated(moving_ref[d * wide + i : d * wide + i + 1, here]) for d in range(COMPS)]
            for c in range(COMPS):
                for j in range(0, main, PACK):
                    prod_ref[i * main + j : i * main + j + PACK, lanes(c)] = along(moving, slopes[c, j])
        if plan.rest:
            moving = {
                i: [moving_ref[d * wide + i : d * wide + i + PACK, here].astype(jnp.bfloat16) for d in range(COMPS)]
                for i in range(0, wide, PACK)
            }
            for c in range(COMPS):
                for j in range(plan.rest):
                    slope = [repeated(row_ref[c * 8 + j : c * 8 + j + 1, there(d)]) for d in range(COMPS)]
                    for i in range(0, wide, PACK):
                        at = plan.pairs + j * wide + i
                        prod_ref[at : at + PACK, lanes(c)] = along(moving[i], slope)

    def multiply(slot, prod_ref, cut):
        low, high = cut
        result = jnp.dot(table_ref[...], prod_ref[:, low:high], preferred_element_type=jnp.float32)
        for at in range(low, high, LANES):
            v, c = divmod(at // LANES, COMPS)
            conv_ref[slot, v, c * pad : (c + 1) * pad, :] = result[:, at - low : at - low + LANES]

    prepare(field_refs[0], 0)
    for p in range(planes):
        cuts = list(plan.cuts) if p else []
        if p + 1 < planes:
            prepare(field_refs[(p + 1) % 2], p + 1)
        for v in range(inner):
            if cuts:
                multiply(p - 1, prod_refs[(p - 1) % 2], cuts.pop(0))
            fill(prod_refs[p % 2], field_refs[p % 2], v)
        for cut in cuts:
            multiply(p - 1, prod_refs[(p - 1) % 2], cut)
    for cut in plan.cuts:
        multiply(planes - 1, prod_refs[(planes - 1) % 2], cut)
    for p in range(planes):
        stacked = jnp.concatenate([conv_ref[p, v].astype(jnp.bfloat16) for v in range(inner)], axis=1)
        placed = jnp.dot(place_ref[...], stacked, preferred_element_type=jnp.float32).astype(jnp.bfloat16)
        for v in range(inner):
            block = placed[:, v * LANES : (v + 1) * LANES]
            out_ref[p, :, v] = block.reshape(plan.chunks, plan.packed, LANES)


def finish_kernel(plan, got_ref, base_ref, swap_ref, conv_ref, next_ref, flat_ref, conv_vmem, next_vmem, sems):
    for v in range(plan.inner):
        parts = [got_ref[s, :, v].reshape(plan.wide, LANES) for s in range(plan.planes)]
        swapped = jnp.dot(jnp.concatenate(parts, axis=1), swap_ref[...], preferred_element_type=jnp.float32)
        for block in range(min(plan.planes, plan.rows - v * plan.planes)):
            for chunk in range(plan.chunks):
                at = (chunk * plan.rows + v * plan.planes + block) * plan.packed
                flat_ref[at : at + plan.packed, :] = swapped[
                    chunk * plan.packed : (chunk + 1) * plan.packed, block * LANES : (block + 1) * LANES
                ]
    copies = []
    for s in range(plan.slot_dev):
        fields = slice(s * COMPS, (s + 1) * COMPS)
        for f in range(s * COMPS, (s + 1) * COMPS):
            value = flat_ref[pl.ds(f, plan.ny, stride=plan.packed), :]
            conv_vmem[f] = value
            next_vmem[f] = base_ref[f] - SECTION_STEP * value
        for which, (source, target) in enumerate(((conv_vmem, conv_ref), (next_vmem, next_ref))):
            copies.append(pltpu.make_async_copy(source.at[fields], target.at[fields], sems.at[which, s]))
            copies[-1].start()
    for copy in copies:
        copy.wait()


def on_device(velocity, base_velocity, mode_slot, triples, triple_coef):
    slot_dev, _, _, ny, nz = velocity.shape
    chunks, planes = lax.axis_size("chaos"), lax.axis_size("space")
    plan = Plan(slot_dev, ny, nz, planes, chunks, mode_slot.shape[0])
    fields, packed, devices = plan.fields, plan.packed, planes * chunks

    def exchange(block):
        flat = block.reshape((devices,) + block.shape[2:])
        return lax.all_to_all(flat, ("space", "chaos"), 0, 0, tiled=True).reshape(block.shape)

    sent = pl.pallas_call(
        functools.partial(pack_kernel, plan),
        out_shape=jax.ShapeDtypeStruct((planes, chunks, plan.vectors, packed, LANES), jnp.bfloat16),
        in_specs=[pl.BlockSpec(memory_space=pltpu.HBM)],
        out_specs=pl.BlockSpec(memory_space=pltpu.HBM),
        scratch_shapes=[
            pltpu.VMEM((fields * ny, nz), jnp.float32),
            pltpu.VMEM((planes, chunks, plan.vectors, packed, LANES), jnp.bfloat16),
            pltpu.SemaphoreType.DMA,
            pltpu.SemaphoreType.DMA((plan.vectors,)),
        ],
        compiler_params=params(PACK_VMEM_LIMIT),
        name="pack",
    )(velocity.reshape(fields * ny, nz))
    got = exchange(sent)
    table, pick, place, swap = pl.pallas_call(
        functools.partial(prepare_kernel, plan),
        out_shape=[
            jax.ShapeDtypeStruct((plan.mode_pad, plan.depth), jnp.bfloat16),
            jax.ShapeDtypeStruct((COMPS * plan.wide_pad, plan.wide), jnp.bfloat16),
            jax.ShapeDtypeStruct((plan.wide, COMPS * plan.mode_pad), jnp.bfloat16),
            jax.ShapeDtypeStruct((planes * LANES, planes * LANES), jnp.bfloat16),
        ],
        in_specs=[pl.BlockSpec(memory_space=pltpu.SMEM)] + [vmem_spec()] * 2,
        out_specs=[vmem_spec()] * 4,
        compiler_params=params(),
        name="prepare",
    )(mode_slot, triples.T, triple_coef.reshape(1, -1))
    returned = pl.pallas_call(
        functools.partial(contract_kernel, plan),
        out_shape=jax.ShapeDtypeStruct((planes, chunks, plan.inner, packed, LANES), jnp.bfloat16),
        in_specs=[vmem_spec()] * 5,
        out_specs=vmem_spec(),
        scratch_shapes=[
            pltpu.VMEM((planes, plan.inner, COMPS * plan.mode_pad, LANES), jnp.float32),
            pltpu.VMEM((planes * plan.wide, 2 * plan.inner * LANES), jnp.bfloat16),
            pltpu.VMEM((plan.depth, plan.lanes), jnp.bfloat16),
            pltpu.VMEM((plan.depth, plan.lanes), jnp.bfloat16),
        ]
        + [
            pltpu.VMEM((COMPS * plan.wide_pad, plan.inner * LANES), jnp.float32),
            pltpu.VMEM((COMPS * 8, plan.lanes), jnp.float32),
            pltpu.VMEM((COMPS * plan.wide_pad, plan.lanes), jnp.bfloat16),
        ]
        * 2,
        compiler_params=params(),
        name="contract",
    )(got, jnp.asarray(plan.stencil(), jnp.bfloat16), table, pick, place)
    convection, next_velocity = pl.pallas_call(
        functools.partial(finish_kernel, plan),
        out_shape=[jax.ShapeDtypeStruct((fields, ny, nz), jnp.float32)] * 2,
        in_specs=[vmem_spec()] * 3,
        out_specs=[pl.BlockSpec(memory_space=pl.ANY)] * 2,
        scratch_shapes=[
            pltpu.VMEM((ny * packed, LANES), jnp.float32),
            pltpu.VMEM((fields, ny, nz), jnp.float32),
            pltpu.VMEM((fields, ny, nz), jnp.float32),
            pltpu.SemaphoreType.DMA((2, slot_dev)),
        ],
        compiler_params=params(),
        name="finish",
    )(exchange(returned), base_velocity.reshape(fields, ny, nz), swap)
    return convection.reshape(velocity.shape), next_velocity.reshape(velocity.shape)


def solution(mesh):
    spread = P("chaos", None, "space", None, None)
    return jax.shard_map(
        on_device,
        mesh=mesh,
        in_specs=(spread, spread, P(), P(), P()),
        out_specs=(spread, spread),
        check_vma=False,
    )
```

```python
import functools

import jax
import jax.numpy as jnp
import numpy as np
from jax import lax
from jax.experimental import pallas as pl
from jax.experimental.pallas import tpu as pltpu
from jax.sharding import PartitionSpec as P

SECTION_STEP = 0.5
COMPS = 3
LANES = 128
LANE_BITS = 7
TILE = 256
PACK = 16
VMEM_LIMIT = 48 * 1024 * 1024
PACK_VMEM_LIMIT = 65280 * 1024


def round_up(value, unit):
    return -(-value // unit) * unit


def vmem_spec():
    return pl.BlockSpec(memory_space=pltpu.VMEM)


def params(limit=VMEM_LIMIT):
    return pltpu.CompilerParams(vmem_limit_bytes=limit)


class Plan:
    def __init__(self, slot_dev, ny, nz, planes, chunks, modes):
        self.slot_dev, self.ny, self.planes, self.chunks, self.modes = slot_dev, ny, planes, chunks, modes
        self.fields = slot_dev * COMPS
        self.packed = round_up(self.fields, 16)
        self.wide = chunks * self.packed
        self.rows = ny // chunks
        self.width = nz // planes
        assert nz == LANES and self.width * planes == nz and self.rows * chunks == ny
        self.width_bits = self.width.bit_length() - 1
        assert self.rest_fits(modes)
        assert planes & (planes - 1) == 0 and 2 * self.rows <= self.width
        self.inner = -(-self.rows // planes)
        if self.rows % planes == 0:
            assert planes >= 3
            self.vectors = self.inner + 1
            first = self.inner * planes
            self.low, self.high, self.side = first, first + 1, first + 2
        else:
            assert self.rows + 3 <= planes
            self.vectors = 1
            self.low, self.high, self.side = planes - 1, self.rows, self.rows + 1
        self.mode_pad = round_up(modes, 8)
        self.main = modes // 16 * 16
        self.rest = modes - self.main
        self.wide_pad = round_up(modes, PACK)
        self.rest_rows = self.rest * self.wide_pad
        self.pairs = modes * self.main
        self.depth = round_up(self.pairs + self.rest_rows, TILE)
        self.groups = self.depth // TILE
        self.lanes = self.inner * COMPS * LANES
        self.cuts = [(at, min(at + TILE, self.lanes)) for at in range(0, self.lanes, TILE)]

    @staticmethod
    def rest_fits(modes):
        return modes >= PACK and modes % PACK <= 8

    def stencil(self):
        out = np.zeros((self.vectors * LANES, 2 * self.inner * LANES), np.float32)
        width = self.width
        for r in range(self.rows):
            above = r + 1 if r + 1 < self.rows else self.high
            below = r - 1 if r > 0 else self.low
            for w in range(width):
                at = r * width + w
                out[above * width + w, at] += 0.5
                out[below * width + w, at] -= 0.5
                right = at + 1 if w + 1 < width else self.side * width + 2 * r + 1
                left = at - 1 if w > 0 else self.side * width + 2 * r
                out[right, self.inner * LANES + at] += 0.5
                out[left, self.inner * LANES + at] -= 0.5
        return out


def block_transposer(plan):
    shape = (plan.planes * LANES, LANES)
    source = lax.broadcasted_iota(jnp.int32, shape, 0)
    target = lax.broadcasted_iota(jnp.int32, shape, 1)
    part, lane = source >> LANE_BITS, source & (LANES - 1)
    block, inner = lane >> plan.width_bits, lane & (plan.width - 1)
    wanted = (block << LANE_BITS) + (part << plan.width_bits) + inner
    return jnp.concatenate(
        [jnp.where(wanted == target + b * LANES, 1.0, 0.0).astype(jnp.bfloat16) for b in range(plan.planes)], axis=1
    )


def side_collector(plan):
    source = lax.broadcasted_iota(jnp.int32, (plan.rows * LANES, LANES), 0)
    target = lax.broadcasted_iota(jnp.int32, (1, LANES), 1)
    block, inner = target >> plan.width_bits, target & (plan.width - 1)
    beside = (block << plan.width_bits) - 1 + (inner & 1) * (plan.width + 1)
    wanted = ((inner >> 1) << LANE_BITS) + (beside & (LANES - 1))
    wanted = jnp.where(inner < 2 * plan.rows, wanted, -1)
    return jnp.where(source == wanted, 1.0, 0.0).astype(jnp.bfloat16)


def pack_kernel(plan, v_hbm, out_hbm, v_ref, out_ref, in_sem, out_sems):
    planes, rows, chunks, packed = plan.planes, plan.rows, plan.chunks, plan.packed
    fetch = pltpu.make_async_copy(v_hbm, v_ref, in_sem)
    fetch.start()
    transposer = block_transposer(plan)
    collector = side_collector(plan)
    fetch.wait()
    pad = jnp.zeros((packed - plan.fields, LANES), jnp.float32)
    lines = []
    for y in range(plan.ny):
        block = v_ref[pl.ds(y, plan.fields, stride=plan.ny), :]
        lines.append(jnp.concatenate([block, pad], axis=0).astype(jnp.bfloat16))

    def across(offset):
        return jnp.concatenate([lines[(c * rows + offset) % plan.ny] for c in range(chunks)], axis=0)

    inside = [across(r) for r in range(rows)]
    side = jnp.dot(jnp.concatenate(inside, axis=1), collector, preferred_element_type=jnp.float32)
    blocks = inside + [jnp.zeros_like(inside[0])] * (plan.vectors * planes - rows)
    blocks[plan.low] = across(-1)
    blocks[plan.high] = across(rows)
    blocks[plan.side] = side.astype(jnp.bfloat16)
    copies = []
    for part in (range(plan.inner), range(plan.inner, plan.vectors)):
        if not part:
            continue
        row = jnp.concatenate(
            [jnp.concatenate(blocks[v * planes : (v + 1) * planes], axis=1) for v in part], axis=0
        )
        swapped = jnp.dot(row, transposer, preferred_element_type=jnp.float32).astype(jnp.bfloat16)
        for at, v in enumerate(part):
            for s in range(planes):
                for c in range(chunks):
                    first = at * plan.wide + c * packed
                    out_ref[s, c, v] = swapped[first : first + packed, s * LANES : (s + 1) * LANES]
            copies.append(pltpu.make_async_copy(out_ref.at[:, :, v], out_hbm.at[:, :, v], out_sems.at[v]))
            copies[-1].start()
    for copy in copies:
        copy.wait()


def prepare_kernel(plan, slot_ref, triples_ref, coef_ref, table_ref, pick_ref, place_ref, swap_ref):
    count = triples_ref.shape[1]
    mode_i = triples_ref[0:1, :]
    mode_j = triples_ref[1:2, :]
    mode_k = triples_ref[2:3, :]
    place = jnp.where(
        mode_j < plan.main,
        mode_i * plan.main + mode_j,
        plan.pairs + (mode_j - plan.main) * plan.wide_pad + mode_i,
    )
    row = (place // TILE) * plan.mode_pad + mode_k
    column = place % TILE
    coef = coef_ref[...].astype(jnp.float32)
    height = plan.groups * plan.mode_pad
    total = jnp.zeros((height, TILE), jnp.float32)
    step = 1024 if count % 1024 == 0 else count
    row_iota = lax.broadcasted_iota(jnp.int32, (height, step), 0)
    column_iota = lax.broadcasted_iota(jnp.int32, (TILE, step), 0)
    for start in range(0, count, step):
        part = slice(start, start + step)
        left = jnp.where(row_iota == row[:, part], coef[:, part], 0.0).astype(jnp.bfloat16)
        right = jnp.where(column_iota == column[:, part], 1.0, 0.0).astype(jnp.bfloat16)
        total = total + lax.dot_general(
            left, right, (((1,), (1,)), ((), ())), preferred_element_type=jnp.float32
        )
    for g in range(plan.groups):
        table_ref[:, g * TILE : (g + 1) * TILE] = total[g * plan.mode_pad : (g + 1) * plan.mode_pad].astype(jnp.bfloat16)

    shape = (plan.wide_pad, plan.wide)
    column = lax.broadcasted_iota(jnp.int32, shape, 1)
    mode = lax.broadcasted_iota(jnp.int32, shape, 0)
    inner = column % plan.packed
    slot = jnp.where(
        inner < plan.fields, (column // plan.packed) * plan.slot_dev + inner // COMPS, -1
    )
    wanted = jnp.full(shape, -2, jnp.int32)
    for m in range(plan.modes):
        wanted = jnp.where(mode == m, slot_ref[m], wanted)
    hit = jnp.where(wanted == slot, 1.0, 0.0)
    pickers = [jnp.where(inner % COMPS == d, hit, 0.0) for d in range(COMPS)]
    pick_ref[...] = jnp.concatenate(pickers, axis=0).astype(jnp.bfloat16)
    narrow = jnp.concatenate([picker[: plan.mode_pad] for picker in pickers], axis=0)
    place_ref[...] = narrow.T.astype(jnp.bfloat16)
    swap_ref[...] = block_transposer(plan)


def contract_kernel(plan, got_ref, stencil_ref, table_ref, pick_ref, place_ref, out_ref, *scratch):
    conv_ref, beside_ref = scratch[:2]
    prod_refs, field_refs = scratch[2:4], (scratch[4:7], scratch[7:10])
    planes, inner, pad, main, wide = plan.planes, plan.inner, plan.mode_pad, plan.main, plan.wide_pad
    tail = plan.pairs + plan.rest_rows
    if tail < plan.depth:
        for ref in prod_refs:
            ref[tail:, :] = jnp.zeros((plan.depth - tail, ref.shape[1]), jnp.bfloat16)

    def vector(p, v):
        return got_ref[p % planes, :, v].reshape(plan.wide, LANES)

    centers = [jnp.concatenate([vector(p, v) for v in range(plan.vectors)], axis=1) for p in range(planes)]
    beside_ref[...] = jnp.dot(
        jnp.concatenate(centers, axis=0), stencil_ref[...], preferred_element_type=jnp.float32
    ).astype(jnp.bfloat16)

    def prepare(fields, p):
        moving_ref, row_ref, slope_ref = fields
        parts = [vector(p, v) for v in range(inner)]
        for v in range(inner):
            ahead, behind = vector(p + 1, v), vector(p - 1, v)
            parts.append((0.5 * (ahead.astype(jnp.float32) - behind.astype(jnp.float32))).astype(jnp.bfloat16))
        parts.append(beside_ref[p * plan.wide : (p + 1) * plan.wide, :])
        picked = jnp.dot(pick_ref[...], jnp.concatenate(parts, axis=1), preferred_element_type=jnp.float32)
        moving_ref[...] = picked[:, : inner * LANES]
        slopes = picked[:, inner * LANES :]
        slope_ref[...] = slopes.astype(jnp.bfloat16)
        for c in range(COMPS):
            row_ref[c * 8 : (c + 1) * 8] = slopes[c * wide + main : c * wide + main + 8]

    def repeated(row):
        return jnp.broadcast_to(row, (PACK, LANES)).astype(jnp.bfloat16)

    def along(left, right):
        term = left[0] * right[0]
        for d in range(1, COMPS):
            term = term + left[d] * right[d]
        return term

    def fill(prod_ref, fields, v):
        moving_ref, row_ref, slope_ref = fields
        here = slice(v * LANES, (v + 1) * LANES)

        def there(d):
            return slice((d * inner + v) * LANES, (d * inner + v + 1) * LANES)

        def lanes(c):
            return slice((v * COMPS + c) * LANES, (v * COMPS + c + 1) * LANES)

        slopes = {
            (c, j): [slope_ref[c * wide + j : c * wide + j + PACK, there(d)] for d in range(COMPS)]
            for c in range(COMPS)
            for j in range(0, main, PACK)
        }
        for i in range(plan.modes):
            moving = [repeated(moving_ref[d * wide + i : d * wide + i + 1, here]) for d in range(COMPS)]
            for c in range(COMPS):
                for j in range(0, main, PACK):
                    prod_ref[i * main + j : i * main + j + PACK, lanes(c)] = along(moving, slopes[c, j])
        if plan.rest:
            moving = {
                i: [moving_ref[d * wide + i : d * wide + i + PACK, here].astype(jnp.bfloat16) for d in range(COMPS)]
                for i in range(0, wide, PACK)
            }
            for c in range(COMPS):
                for j in range(plan.rest):
                    slope = [repeated(row_ref[c * 8 + j : c * 8 + j + 1, there(d)]) for d in range(COMPS)]
                    for i in range(0, wide, PACK):
                        at = plan.pairs + j * wide + i
                        prod_ref[at : at + PACK, lanes(c)] = along(moving[i], slope)

    def multiply(slot, prod_ref, cut):
        low, high = cut
        result = jnp.dot(table_ref[...], prod_ref[:, low:high], preferred_element_type=jnp.float32)
        for at in range(low, high, LANES):
            v, c = divmod(at // LANES, COMPS)
            conv_ref[slot, v, c * pad : (c + 1) * pad, :] = result[:, at - low : at - low + LANES]

    prepare(field_refs[0], 0)
    ready = []
    for p in range(planes):
        if p + 1 < planes:
            prepare(field_refs[(p + 1) % 2], p + 1)
        for v in range(inner):
            while ready:
                multiply(*ready.pop(0))
            fill(prod_refs[p % 2], field_refs[p % 2], v)
            done, filled = v * COMPS * LANES, (v + 1) * COMPS * LANES
            ready = [(p, prod_refs[p % 2], cut) for cut in plan.cuts if done < cut[1] <= filled]
    while ready:
        multiply(*ready.pop(0))
    for p in range(planes):
        stacked = jnp.concatenate([conv_ref[p, v].astype(jnp.bfloat16) for v in range(inner)], axis=1)
        placed = jnp.dot(place_ref[...], stacked, preferred_element_type=jnp.float32).astype(jnp.bfloat16)
        for v in range(inner):
            block = placed[:, v * LANES : (v + 1) * LANES]
            out_ref[p, :, v] = block.reshape(plan.chunks, plan.packed, LANES)


def finish_kernel(plan, got_ref, base_ref, swap_ref, conv_ref, next_ref, flat_ref, conv_vmem, next_vmem, sems):
    rows = [
        jnp.concatenate([got_ref[s, :, v].reshape(plan.wide, LANES) for s in range(plan.planes)], axis=1)
        for v in range(plan.inner)
    ]
    swapped = jnp.dot(jnp.concatenate(rows, axis=0), swap_ref[...], preferred_element_type=jnp.float32)
    for v in range(plan.inner):
        for block in range(min(plan.planes, plan.rows - v * plan.planes)):
            for chunk in range(plan.chunks):
                at = (chunk * plan.rows + v * plan.planes + block) * plan.packed
                first = v * plan.wide + chunk * plan.packed
                flat_ref[at : at + plan.packed, :] = swapped[
                    first : first + plan.packed, block * LANES : (block + 1) * LANES
                ]
    copies = []
    for s in range(plan.slot_dev):
        fields = slice(s * COMPS, (s + 1) * COMPS)
        for f in range(s * COMPS, (s + 1) * COMPS):
            value = flat_ref[pl.ds(f, plan.ny, stride=plan.packed), :]
            conv_vmem[f] = value
            next_vmem[f] = base_ref[f] - SECTION_STEP * value
        for which, (source, target) in enumerate(((conv_vmem, conv_ref), (next_vmem, next_ref))):
            copies.append(pltpu.make_async_copy(source.at[fields], target.at[fields], sems.at[which, s]))
            copies[-1].start()
    for copy in copies:
        copy.wait()


def on_device(velocity, base_velocity, mode_slot, triples, triple_coef):
    slot_dev, _, _, ny, nz = velocity.shape
    chunks, planes = lax.axis_size("chaos"), lax.axis_size("space")
    plan = Plan(slot_dev, ny, nz, planes, chunks, mode_slot.shape[0])
    fields, packed, devices = plan.fields, plan.packed, planes * chunks

    def exchange(block):
        flat = block.reshape((devices,) + block.shape[2:])
        return lax.all_to_all(flat, ("space", "chaos"), 0, 0, tiled=True).reshape(block.shape)

    sent = pl.pallas_call(
        functools.partial(pack_kernel, plan),
        out_shape=jax.ShapeDtypeStruct((planes, chunks, plan.vectors, packed, LANES), jnp.bfloat16),
        in_specs=[pl.BlockSpec(memory_space=pltpu.HBM)],
        out_specs=pl.BlockSpec(memory_space=pltpu.HBM),
        scratch_shapes=[
            pltpu.VMEM((fields * ny, nz), jnp.float32),
            pltpu.VMEM((planes, chunks, plan.vectors, packed, LANES), jnp.bfloat16),
            pltpu.SemaphoreType.DMA,
            pltpu.SemaphoreType.DMA((plan.vectors,)),
        ],
        compiler_params=params(PACK_VMEM_LIMIT),
        name="pack",
    )(velocity.reshape(fields * ny, nz))
    got = exchange(sent)
    table, pick, place, swap = pl.pallas_call(
        functools.partial(prepare_kernel, plan),
        out_shape=[
            jax.ShapeDtypeStruct((plan.mode_pad, plan.depth), jnp.bfloat16),
            jax.ShapeDtypeStruct((COMPS * plan.wide_pad, plan.wide), jnp.bfloat16),
            jax.ShapeDtypeStruct((plan.wide, COMPS * plan.mode_pad), jnp.bfloat16),
            jax.ShapeDtypeStruct((planes * LANES, planes * LANES), jnp.bfloat16),
        ],
        in_specs=[pl.BlockSpec(memory_space=pltpu.SMEM)] + [vmem_spec()] * 2,
        out_specs=[vmem_spec()] * 4,
        compiler_params=params(),
        name="prepare",
    )(mode_slot, triples.T, triple_coef.reshape(1, -1))
    returned = pl.pallas_call(
        functools.partial(contract_kernel, plan),
        out_shape=jax.ShapeDtypeStruct((planes, chunks, plan.inner, packed, LANES), jnp.bfloat16),
        in_specs=[vmem_spec()] * 5,
        out_specs=vmem_spec(),
        scratch_shapes=[
            pltpu.VMEM((planes, plan.inner, COMPS * plan.mode_pad, LANES), jnp.float32),
            pltpu.VMEM((planes * plan.wide, 2 * plan.inner * LANES), jnp.bfloat16),
            pltpu.VMEM((plan.depth, plan.lanes), jnp.bfloat16),
            pltpu.VMEM((plan.depth, plan.lanes), jnp.bfloat16),
        ]
        + [
            pltpu.VMEM((COMPS * plan.wide_pad, plan.inner * LANES), jnp.float32),
            pltpu.VMEM((COMPS * 8, plan.lanes), jnp.float32),
            pltpu.VMEM((COMPS * plan.wide_pad, plan.lanes), jnp.bfloat16),
        ]
        * 2,
        compiler_params=params(),
        name="contract",
    )(got, jnp.asarray(plan.stencil(), jnp.bfloat16), table, pick, place)
    convection, next_velocity = pl.pallas_call(
        functools.partial(finish_kernel, plan),
        out_shape=[jax.ShapeDtypeStruct((fields, ny, nz), jnp.float32)] * 2,
        in_specs=[vmem_spec()] * 3,
        out_specs=[pl.BlockSpec(memory_space=pl.ANY)] * 2,
        scratch_shapes=[
            pltpu.VMEM((ny * packed, LANES), jnp.float32),
            pltpu.VMEM((fields, ny, nz), jnp.float32),
            pltpu.VMEM((fields, ny, nz), jnp.float32),
            pltpu.SemaphoreType.DMA((2, slot_dev)),
        ],
        compiler_params=params(),
        name="finish",
    )(exchange(returned), base_velocity.reshape(fields, ny, nz), swap)
    return convection.reshape(velocity.shape), next_velocity.reshape(velocity.shape)


def solution(mesh):
    spread = P("chaos", None, "space", None, None)
    return jax.shard_map(
        on_device,
        mesh=mesh,
        in_specs=(spread, spread, P(), P(), P()),
        out_specs=(spread, spread),
        check_vma=False,
    )
```

```python
import functools

import jax
import jax.numpy as jnp
import numpy as np
from jax import lax
from jax.experimental import pallas as pl
from jax.experimental.pallas import tpu as pltpu
from jax.sharding import PartitionSpec as P

SECTION_STEP = 0.5
COMPS = 3
LANES = 128
LANE_BITS = 7
TILE = 256
PACK = 16
VMEM_LIMIT = 48 * 1024 * 1024
PACK_VMEM_LIMIT = 65280 * 1024


def round_up(value, unit):
    return -(-value // unit) * unit


def vmem_spec():
    return pl.BlockSpec(memory_space=pltpu.VMEM)


def params(limit=VMEM_LIMIT):
    return pltpu.CompilerParams(vmem_limit_bytes=limit)


class Plan:
    def __init__(self, slot_dev, ny, nz, planes, chunks, modes):
        self.slot_dev, self.ny, self.planes, self.chunks, self.modes = slot_dev, ny, planes, chunks, modes
        self.fields = slot_dev * COMPS
        self.packed = round_up(self.fields, 16)
        self.wide = chunks * self.packed
        self.rows = ny // chunks
        self.width = nz // planes
        assert nz == LANES and self.width * planes == nz and self.rows * chunks == ny
        self.width_bits = self.width.bit_length() - 1
        assert self.rest_fits(modes)
        assert planes & (planes - 1) == 0 and 2 * self.rows <= self.width
        self.inner = -(-self.rows // planes)
        if self.rows % planes == 0:
            assert planes >= 3
            self.vectors = self.inner + 1
            first = self.inner * planes
            self.low, self.high, self.side = first, first + 1, first + 2
        else:
            assert self.rows + 3 <= planes
            self.vectors = 1
            self.low, self.high, self.side = planes - 1, self.rows, self.rows + 1
        self.mode_pad = round_up(modes, 8)
        self.main = modes // 16 * 16
        self.rest = modes - self.main
        self.wide_pad = round_up(modes, PACK)
        self.rest_rows = self.rest * self.wide_pad
        self.pairs = modes * self.main
        self.depth = round_up(self.pairs + self.rest_rows, TILE)
        self.groups = self.depth // TILE
        self.lanes = 2 * COMPS * LANES
        self.cuts = [(at, at + TILE) for at in range(0, self.lanes, TILE)]
        if self.inner == 2 and self.vectors == 3 and planes >= 4:
            self.copy = self.side + 1
            self.sends = [[0, 2], [1]]
            self.turns = [([0], [0, 2]), ([1], [0, 2, 1])]
        else:
            self.copy = None
            self.sends = [list(range(self.vectors))]
            self.turns = [(list(range(self.inner)), list(range(self.vectors)))]

    @staticmethod
    def rest_fits(modes):
        return modes >= PACK and modes % PACK <= 8

    def stencil(self, own, order):
        out = np.zeros((len(order) * LANES, 2 * len(own) * LANES), np.float32)

        def lane(block):
            vector, part = divmod(block, self.planes)
            if vector not in order:
                return lane(self.copy)
            return order.index(vector) * LANES + part * self.width

        for r in range(self.rows):
            if r // self.planes not in own:
                continue
            above = lane(r + 1 if r + 1 < self.rows else self.high)
            below = lane(r - 1 if r > 0 else self.low)
            here = lane(r)
            first = own.index(r // self.planes) * LANES + r % self.planes * self.width
            for w in range(self.width):
                out[above + w, first + w] += 0.5
                out[below + w, first + w] -= 0.5
                right = here + w + 1 if w + 1 < self.width else lane(self.side) + 2 * r + 1
                left = here + w - 1 if w > 0 else lane(self.side) + 2 * r
                out[right, len(own) * LANES + first + w] += 0.5
                out[left, len(own) * LANES + first + w] -= 0.5
        return out


def block_transposer(plan):
    shape = (plan.planes * LANES, LANES)
    source = lax.broadcasted_iota(jnp.int32, shape, 0)
    target = lax.broadcasted_iota(jnp.int32, shape, 1)
    part, lane = source >> LANE_BITS, source & (LANES - 1)
    block, inner = lane >> plan.width_bits, lane & (plan.width - 1)
    wanted = (block << LANE_BITS) + (part << plan.width_bits) + inner
    return jnp.concatenate(
        [jnp.where(wanted == target + b * LANES, 1.0, 0.0).astype(jnp.bfloat16) for b in range(plan.planes)], axis=1
    )


def side_collector(plan):
    source = lax.broadcasted_iota(jnp.int32, (plan.rows * LANES, LANES), 0)
    target = lax.broadcasted_iota(jnp.int32, (1, LANES), 1)
    block, inner = target >> plan.width_bits, target & (plan.width - 1)
    beside = (block << plan.width_bits) - 1 + (inner & 1) * (plan.width + 1)
    wanted = ((inner >> 1) << LANE_BITS) + (beside & (LANES - 1))
    wanted = jnp.where(inner < 2 * plan.rows, wanted, -1)
    return jnp.where(source == wanted, 1.0, 0.0).astype(jnp.bfloat16)


def pack_kernel(plan, v_hbm, *refs):
    out_hbms, (v_ref, out_ref, in_sem, out_sems) = refs[: len(plan.sends)], refs[len(plan.sends) :]
    planes, rows, chunks, packed = plan.planes, plan.rows, plan.chunks, plan.packed
    fetch = pltpu.make_async_copy(v_hbm, v_ref, in_sem)
    fetch.start()
    transposer = block_transposer(plan)
    collector = side_collector(plan)
    fetch.wait()
    pad = jnp.zeros((packed - plan.fields, LANES), jnp.float32)
    lines = []
    for y in range(plan.ny):
        block = v_ref[pl.ds(y, plan.fields, stride=plan.ny), :]
        lines.append(jnp.concatenate([block, pad], axis=0).astype(jnp.bfloat16))

    def across(offset):
        return jnp.concatenate([lines[(c * rows + offset) % plan.ny] for c in range(chunks)], axis=0)

    inside = [across(r) for r in range(rows)]
    side = jnp.dot(jnp.concatenate(inside, axis=1), collector, preferred_element_type=jnp.float32)
    blocks = inside + [jnp.zeros_like(inside[0])] * (plan.vectors * planes - rows)
    blocks[plan.low] = across(-1)
    blocks[plan.high] = across(rows)
    blocks[plan.side] = side.astype(jnp.bfloat16)
    if plan.copy is not None:
        blocks[plan.copy] = inside[planes]
    copies = []
    for part in (range(plan.inner), range(plan.inner, plan.vectors)):
        if not part:
            continue
        row = jnp.concatenate(
            [jnp.concatenate(blocks[v * planes : (v + 1) * planes], axis=1) for v in part], axis=0
        )
        swapped = jnp.dot(row, transposer, preferred_element_type=jnp.float32).astype(jnp.bfloat16)
        for at, v in enumerate(part):
            for s in range(planes):
                for c in range(chunks):
                    first = at * plan.wide + c * packed
                    out_ref[s, c, v] = swapped[first : first + packed, s * LANES : (s + 1) * LANES]
            which = [v in send for send in plan.sends].index(True)
            target = out_hbms[which].at[:, :, plan.sends[which].index(v)]
            copies.append(pltpu.make_async_copy(out_ref.at[:, :, v], target, out_sems.at[v]))
            copies[-1].start()
    for copy in copies:
        copy.wait()


def prepare_kernel(plan, slot_ref, triples_ref, coef_ref, table_ref, pick_ref, place_ref, swap_ref):
    count = triples_ref.shape[1]
    mode_i = triples_ref[0:1, :]
    mode_j = triples_ref[1:2, :]
    mode_k = triples_ref[2:3, :]
    place = jnp.where(
        mode_j < plan.main,
        mode_i * plan.main + mode_j,
        plan.pairs + (mode_j - plan.main) * plan.wide_pad + mode_i,
    )
    row = (place // TILE) * plan.mode_pad + mode_k
    column = place % TILE
    coef = coef_ref[...].astype(jnp.float32)
    height = plan.groups * plan.mode_pad
    total = jnp.zeros((height, TILE), jnp.float32)
    step = 1024 if count % 1024 == 0 else count
    row_iota = lax.broadcasted_iota(jnp.int32, (height, step), 0)
    column_iota = lax.broadcasted_iota(jnp.int32, (TILE, step), 0)
    for start in range(0, count, step):
        part = slice(start, start + step)
        left = jnp.where(row_iota == row[:, part], coef[:, part], 0.0).astype(jnp.bfloat16)
        right = jnp.where(column_iota == column[:, part], 1.0, 0.0).astype(jnp.bfloat16)
        total = total + lax.dot_general(
            left, right, (((1,), (1,)), ((), ())), preferred_element_type=jnp.float32
        )
    for g in range(plan.groups):
        table_ref[:, g * TILE : (g + 1) * TILE] = total[g * plan.mode_pad : (g + 1) * plan.mode_pad].astype(jnp.bfloat16)

    shape = (plan.wide_pad, plan.wide)
    column = lax.broadcasted_iota(jnp.int32, shape, 1)
    mode = lax.broadcasted_iota(jnp.int32, shape, 0)
    inner = column % plan.packed
    slot = jnp.where(
        inner < plan.fields, (column // plan.packed) * plan.slot_dev + inner // COMPS, -1
    )
    wanted = jnp.full(shape, -2, jnp.int32)
    for m in range(plan.modes):
        wanted = jnp.where(mode == m, slot_ref[m], wanted)
    hit = jnp.where(wanted == slot, 1.0, 0.0)
    pickers = [jnp.where(inner % COMPS == d, hit, 0.0) for d in range(COMPS)]
    pick_ref[...] = jnp.concatenate(pickers, axis=0).astype(jnp.bfloat16)
    narrow = jnp.concatenate([picker[: plan.mode_pad] for picker in pickers], axis=0)
    place_ref[...] = narrow.T.astype(jnp.bfloat16)
    swap_ref[...] = block_transposer(plan)


def contract_kernel(plan, turn, stencil_ref, table_ref, pick_ref, place_ref, *refs):
    own, order = plan.turns[turn]
    got_refs, refs = refs[: turn + 1], refs[turn + 1 :]
    earlier_refs, refs = refs[: min(turn, 1)], refs[min(turn, 1) :]
    out_ref, conv_ref, beside_ref = refs[:3]
    prod_refs, field_refs = refs[3:5], (refs[5:8], refs[8:11])
    planes, pad, main, wide = plan.planes, plan.mode_pad, plan.main, plan.wide_pad
    count = len(own)
    tail = plan.pairs + plan.rest_rows
    if tail < plan.depth:
        for ref in prod_refs:
            ref[tail:, :] = jnp.zeros((plan.depth - tail, ref.shape[1]), jnp.bfloat16)

    def vector(p, v):
        which = [v in send for send in plan.sends].index(True)
        return got_refs[which][p % planes, :, plan.sends[which].index(v)].reshape(plan.wide, LANES)

    centers = [jnp.concatenate([vector(p, v) for v in order], axis=1) for p in range(planes)]
    beside_ref[...] = jnp.dot(
        jnp.concatenate(centers, axis=0), stencil_ref[...], preferred_element_type=jnp.float32
    ).astype(jnp.bfloat16)
    items = [(p, at) for p in range(planes) for at in range(count)]

    def prepare(fields, item):
        moving_ref, row_ref, slope_ref = fields
        p, at = item
        ahead, behind = vector(p + 1, own[at]), vector(p - 1, own[at])
        parts = [
            vector(p, own[at]),
            (0.5 * (ahead.astype(jnp.float32) - behind.astype(jnp.float32))).astype(jnp.bfloat16),
        ]
        for kind in range(2):
            lanes = slice((kind * count + at) * LANES, (kind * count + at + 1) * LANES)
            parts.append(beside_ref[p * plan.wide : (p + 1) * plan.wide, lanes])
        picked = jnp.dot(pick_ref[...], jnp.concatenate(parts, axis=1), preferred_element_type=jnp.float32)
        moving_ref[...] = picked[:, :LANES]
        slopes = picked[:, LANES:]
        slope_ref[...] = slopes.astype(jnp.bfloat16)
        for c in range(COMPS):
            row_ref[c * 8 : (c + 1) * 8] = slopes[c * wide + main : c * wide + main + 8]

    def repeated(row):
        return jnp.broadcast_to(row, (PACK, LANES)).astype(jnp.bfloat16)

    def along(left, right):
        term = left[0] * right[0]
        for d in range(1, COMPS):
            term = term + left[d] * right[d]
        return term

    def fill(prod_ref, fields, place):
        moving_ref, row_ref, slope_ref = fields
        here = slice(0, LANES)

        def there(d):
            return slice(d * LANES, (d + 1) * LANES)

        def lanes(c):
            return slice((place * COMPS + c) * LANES, (place * COMPS + c + 1) * LANES)

        slopes = {
            (c, j): [slope_ref[c * wide + j : c * wide + j + PACK, there(d)] for d in range(COMPS)]
            for c in range(COMPS)
            for j in range(0, main, PACK)
        }
        for i in range(plan.modes):
            moving = [repeated(moving_ref[d * wide + i : d * wide + i + 1, here]) for d in range(COMPS)]
            for c in range(COMPS):
                for j in range(0, main, PACK):
                    prod_ref[i * main + j : i * main + j + PACK, lanes(c)] = along(moving, slopes[c, j])
        if plan.rest:
            moving = {
                i: [moving_ref[d * wide + i : d * wide + i + PACK, here].astype(jnp.bfloat16) for d in range(COMPS)]
                for i in range(0, wide, PACK)
            }
            for c in range(COMPS):
                for j in range(plan.rest):
                    slope = [repeated(row_ref[c * 8 + j : c * 8 + j + 1, there(d)]) for d in range(COMPS)]
                    for i in range(0, wide, PACK):
                        at = plan.pairs + j * wide + i
                        prod_ref[at : at + PACK, lanes(c)] = along(moving[i], slope)

    def multiply(unit, cut):
        low, high = cut
        prod_ref = prod_refs[unit % 2]
        result = jnp.dot(table_ref[...], prod_ref[:, low:high], preferred_element_type=jnp.float32)
        for lane in range(low, high, LANES):
            place, c = divmod(lane // LANES, COMPS)
            p, at = items[2 * unit + place]
            conv_ref[p, at, c * pad : (c + 1) * pad, :] = result[:, lane - low : lane - low + LANES]

    prepare(field_refs[0], items[0])
    ready = []
    for index in range(len(items)):
        unit, place = divmod(index, 2)
        if index + 1 < len(items):
            prepare(field_refs[(index + 1) % 2], items[index + 1])
        while ready:
            multiply(*ready.pop(0))
        fill(prod_refs[unit % 2], field_refs[index % 2], place)
        done, filled = place * COMPS * LANES, (place + 1) * COMPS * LANES
        ready = [(unit, cut) for cut in plan.cuts if done < cut[1] <= filled]
    while ready:
        multiply(*ready.pop(0))
    for p in range(planes):
        stacked = jnp.concatenate([conv_ref[p, at].astype(jnp.bfloat16) for at in range(count)], axis=1)
        placed = jnp.dot(place_ref[...], stacked, preferred_element_type=jnp.float32).astype(jnp.bfloat16)
        for at in range(count):
            block = placed[:, at * LANES : (at + 1) * LANES]
            out_ref[p, :, turn + at] = block.reshape(plan.chunks, plan.packed, LANES)
        for ref in earlier_refs:
            out_ref[p, :, :turn] = ref[p]


def finish_kernel(plan, got_ref, base_ref, swap_ref, conv_ref, next_ref, flat_ref, conv_vmem, next_vmem, sems):
    rows = [
        jnp.concatenate([got_ref[s, :, v].reshape(plan.wide, LANES) for s in range(plan.planes)], axis=1)
        for v in range(plan.inner)
    ]
    swapped = jnp.dot(jnp.concatenate(rows, axis=0), swap_ref[...], preferred_element_type=jnp.float32)
    for v in range(plan.inner):
        for block in range(min(plan.planes, plan.rows - v * plan.planes)):
            for chunk in range(plan.chunks):
                at = (chunk * plan.rows + v * plan.planes + block) * plan.packed
                first = v * plan.wide + chunk * plan.packed
                flat_ref[at : at + plan.packed, :] = swapped[
                    first : first + plan.packed, block * LANES : (block + 1) * LANES
                ]
    copies = []
    for s in range(plan.slot_dev):
        fields = slice(s * COMPS, (s + 1) * COMPS)
        for f in range(s * COMPS, (s + 1) * COMPS):
            value = flat_ref[pl.ds(f, plan.ny, stride=plan.packed), :]
            conv_vmem[f] = value
            next_vmem[f] = base_ref[f] - SECTION_STEP * value
        for which, (source, target) in enumerate(((conv_vmem, conv_ref), (next_vmem, next_ref))):
            copies.append(pltpu.make_async_copy(source.at[fields], target.at[fields], sems.at[which, s]))
            copies[-1].start()
    for copy in copies:
        copy.wait()


def on_device(velocity, base_velocity, mode_slot, triples, triple_coef):
    slot_dev, _, _, ny, nz = velocity.shape
    chunks, planes = lax.axis_size("chaos"), lax.axis_size("space")
    plan = Plan(slot_dev, ny, nz, planes, chunks, mode_slot.shape[0])
    fields, packed, devices = plan.fields, plan.packed, planes * chunks

    def exchange(block):
        flat = block.reshape((devices,) + block.shape[2:])
        return lax.all_to_all(flat, ("space", "chaos"), 0, 0, tiled=True).reshape(block.shape)

    sent = pl.pallas_call(
        functools.partial(pack_kernel, plan),
        out_shape=[
            jax.ShapeDtypeStruct((planes, chunks, len(send), packed, LANES), jnp.bfloat16) for send in plan.sends
        ],
        in_specs=[pl.BlockSpec(memory_space=pltpu.HBM)],
        out_specs=[pl.BlockSpec(memory_space=pltpu.HBM)] * len(plan.sends),
        scratch_shapes=[
            pltpu.VMEM((fields * ny, nz), jnp.float32),
            pltpu.VMEM((planes, chunks, plan.vectors, packed, LANES), jnp.bfloat16),
            pltpu.SemaphoreType.DMA,
            pltpu.SemaphoreType.DMA((plan.vectors,)),
        ],
        compiler_params=params(PACK_VMEM_LIMIT),
        name="pack",
    )(velocity.reshape(fields * ny, nz))
    got = [exchange(block) for block in sent]
    table, pick, place, swap = pl.pallas_call(
        functools.partial(prepare_kernel, plan),
        out_shape=[
            jax.ShapeDtypeStruct((plan.mode_pad, plan.depth), jnp.bfloat16),
            jax.ShapeDtypeStruct((COMPS * plan.wide_pad, plan.wide), jnp.bfloat16),
            jax.ShapeDtypeStruct((plan.wide, COMPS * plan.mode_pad), jnp.bfloat16),
            jax.ShapeDtypeStruct((planes * LANES, planes * LANES), jnp.bfloat16),
        ],
        in_specs=[pl.BlockSpec(memory_space=pltpu.SMEM)] + [vmem_spec()] * 2,
        out_specs=[vmem_spec()] * 4,
        compiler_params=params(),
        name="prepare",
    )(mode_slot, triples.T, triple_coef.reshape(1, -1))
    returned = []
    for turn, (own, order) in enumerate(plan.turns):
        stencil = jnp.asarray(plan.stencil(own, order), jnp.bfloat16)
        returned = [
            pl.pallas_call(
                functools.partial(contract_kernel, plan, turn),
                out_shape=jax.ShapeDtypeStruct((planes, chunks, turn + len(own), packed, LANES), jnp.bfloat16),
                in_specs=[vmem_spec()] * (5 + turn + len(returned)),
                out_specs=vmem_spec(),
                scratch_shapes=[
                    pltpu.VMEM((planes, len(own), COMPS * plan.mode_pad, LANES), jnp.float32),
                    pltpu.VMEM((planes * plan.wide, 2 * len(own) * LANES), jnp.bfloat16),
                    pltpu.VMEM((plan.depth, plan.lanes), jnp.bfloat16),
                    pltpu.VMEM((plan.depth, plan.lanes), jnp.bfloat16),
                ]
                + [
                    pltpu.VMEM((COMPS * plan.wide_pad, LANES), jnp.float32),
                    pltpu.VMEM((COMPS * 8, COMPS * LANES), jnp.float32),
                    pltpu.VMEM((COMPS * plan.wide_pad, COMPS * LANES), jnp.bfloat16),
                ]
                * 2,
                compiler_params=params(),
                cost_estimate=pl.CostEstimate(flops=2_000_000_000, bytes_accessed=1_000_000, transcendentals=0),
                name="contract",
            )(stencil, table, pick, place, *got[: turn + 1], *returned)
        ]
    convection, next_velocity = pl.pallas_call(
        functools.partial(finish_kernel, plan),
        out_shape=[jax.ShapeDtypeStruct((fields, ny, nz), jnp.float32)] * 2,
        in_specs=[vmem_spec()] * 3,
        out_specs=[pl.BlockSpec(memory_space=pl.ANY)] * 2,
        scratch_shapes=[
            pltpu.VMEM((ny * packed, LANES), jnp.float32),
            pltpu.VMEM((fields, ny, nz), jnp.float32),
            pltpu.VMEM((fields, ny, nz), jnp.float32),
            pltpu.SemaphoreType.DMA((2, slot_dev)),
        ],
        compiler_params=params(),
        name="finish",
    )(exchange(returned[0]), base_velocity.reshape(fields, ny, nz), swap)
    return convection.reshape(velocity.shape), next_velocity.reshape(velocity.shape)


def solution(mesh):
    spread = P("chaos", None, "space", None, None)
    return jax.shard_map(
        on_device,
        mesh=mesh,
        in_specs=(spread, spread, P(), P(), P()),
        out_specs=(spread, spread),
        check_vma=False,
    )
```

```python
import functools

import jax
import jax.numpy as jnp
import numpy as np
from jax import lax
from jax.experimental import pallas as pl
from jax.experimental.pallas import tpu as pltpu
from jax.sharding import PartitionSpec as P

SECTION_STEP = 0.5
COMPS = 3
LANES = 128
LANE_BITS = 7
TILE = 256
PACK = 16
VMEM_LIMIT = 48 * 1024 * 1024
PACK_VMEM_LIMIT = 65280 * 1024


def round_up(value, unit):
    return -(-value // unit) * unit


def vmem_spec():
    return pl.BlockSpec(memory_space=pltpu.VMEM)


def params(limit=VMEM_LIMIT):
    return pltpu.CompilerParams(vmem_limit_bytes=limit)


class Plan:
    def __init__(self, slot_dev, ny, nz, planes, chunks, modes):
        self.slot_dev, self.ny, self.planes, self.chunks, self.modes = slot_dev, ny, planes, chunks, modes
        self.fields = slot_dev * COMPS
        self.packed = round_up(self.fields, 16)
        self.wide = chunks * self.packed
        self.rows = ny // chunks
        self.width = nz // planes
        assert nz == LANES and self.width * planes == nz and self.rows * chunks == ny
        self.width_bits = self.width.bit_length() - 1
        assert self.rest_fits(modes)
        assert planes & (planes - 1) == 0 and 2 * self.rows <= self.width
        self.inner = -(-self.rows // planes)
        if self.rows % planes == 0:
            assert planes >= 3
            self.vectors = self.inner + 1
            first = self.inner * planes
            self.low, self.high, self.side = first, first + 1, first + 2
        else:
            assert self.rows + 3 <= planes
            self.vectors = 1
            self.low, self.high, self.side = planes - 1, self.rows, self.rows + 1
        self.mode_pad = round_up(modes, 8)
        self.main = modes // 16 * 16
        self.rest = modes - self.main
        self.wide_pad = round_up(modes, PACK)
        self.rest_rows = self.rest * self.wide_pad
        self.pairs = modes * self.main
        self.depth = round_up(self.pairs + self.rest_rows, TILE)
        self.groups = self.depth // TILE
        self.lanes = self.inner * COMPS * LANES
        self.cuts = [(at, min(at + TILE, self.lanes)) for at in range(0, self.lanes, TILE)]

    @staticmethod
    def rest_fits(modes):
        return modes >= PACK and modes % PACK <= 8

    def stencil(self):
        out = np.zeros((self.vectors * LANES, 2 * self.inner * LANES), np.float32)
        width = self.width
        for r in range(self.rows):
            above = r + 1 if r + 1 < self.rows else self.high
            below = r - 1 if r > 0 else self.low
            for w in range(width):
                at = r * width + w
                out[above * width + w, at] += 0.5
                out[below * width + w, at] -= 0.5
                right = at + 1 if w + 1 < width else self.side * width + 2 * r + 1
                left = at - 1 if w > 0 else self.side * width + 2 * r
                out[right, self.inner * LANES + at] += 0.5
                out[left, self.inner * LANES + at] -= 0.5
        return out


def block_transposer(plan):
    shape = (plan.planes * LANES, LANES)
    source = lax.broadcasted_iota(jnp.int32, shape, 0)
    target = lax.broadcasted_iota(jnp.int32, shape, 1)
    part, lane = source >> LANE_BITS, source & (LANES - 1)
    block, inner = lane >> plan.width_bits, lane & (plan.width - 1)
    wanted = (block << LANE_BITS) + (part << plan.width_bits) + inner
    return jnp.concatenate(
        [jnp.where(wanted == target + b * LANES, 1.0, 0.0).astype(jnp.bfloat16) for b in range(plan.planes)], axis=1
    )


def side_collector(plan):
    source = lax.broadcasted_iota(jnp.int32, (plan.rows * LANES, LANES), 0)
    target = lax.broadcasted_iota(jnp.int32, (1, LANES), 1)
    block, inner = target >> plan.width_bits, target & (plan.width - 1)
    beside = (block << plan.width_bits) - 1 + (inner & 1) * (plan.width + 1)
    wanted = ((inner >> 1) << LANE_BITS) + (beside & (LANES - 1))
    wanted = jnp.where(inner < 2 * plan.rows, wanted, -1)
    return jnp.where(source == wanted, 1.0, 0.0).astype(jnp.bfloat16)


def pack_kernel(plan, v_hbm, out_hbm, v_ref, out_ref, in_sem, out_sems):
    planes, rows, chunks, packed = plan.planes, plan.rows, plan.chunks, plan.packed
    fetch = pltpu.make_async_copy(v_hbm, v_ref, in_sem)
    fetch.start()
    transposer = block_transposer(plan)
    collector = side_collector(plan)
    fetch.wait()
    pad = jnp.zeros((packed - plan.fields, LANES), jnp.float32)
    lines = []
    for y in range(plan.ny):
        block = v_ref[pl.ds(y, plan.fields, stride=plan.ny), :]
        lines.append(jnp.concatenate([block, pad], axis=0).astype(jnp.bfloat16))

    def across(offset):
        return jnp.concatenate([lines[(c * rows + offset) % plan.ny] for c in range(chunks)], axis=0)

    inside = [across(r) for r in range(rows)]
    side = jnp.dot(jnp.concatenate(inside, axis=1), collector, preferred_element_type=jnp.float32)
    blocks = inside + [jnp.zeros_like(inside[0])] * (plan.vectors * planes - rows)
    blocks[plan.low] = across(-1)
    blocks[plan.high] = across(rows)
    blocks[plan.side] = side.astype(jnp.bfloat16)
    copies = []
    for part in (range(plan.inner), range(plan.inner, plan.vectors)):
        if not part:
            continue
        row = jnp.concatenate(
            [jnp.concatenate(blocks[v * planes : (v + 1) * planes], axis=1) for v in part], axis=0
        )
        swapped = jnp.dot(row, transposer, preferred_element_type=jnp.float32).astype(jnp.bfloat16)
        for at, v in enumerate(part):
            for s in range(planes):
                for c in range(chunks):
                    first = at * plan.wide + c * packed
                    out_ref[s, c, v] = swapped[first : first + packed, s * LANES : (s + 1) * LANES]
            copies.append(pltpu.make_async_copy(out_ref.at[:, :, v], out_hbm.at[:, :, v], out_sems.at[v]))
            copies[-1].start()
    for copy in copies:
        copy.wait()


def prepare_kernel(plan, slot_ref, triples_ref, coef_ref, table_ref, pick_ref, place_ref, swap_ref):
    count = triples_ref.shape[1]
    mode_i = triples_ref[0:1, :]
    mode_j = triples_ref[1:2, :]
    mode_k = triples_ref[2:3, :]
    place = jnp.where(
        mode_j < plan.main,
        mode_i * plan.main + mode_j,
        plan.pairs + (mode_j - plan.main) * plan.wide_pad + mode_i,
    )
    row = (place // TILE) * plan.mode_pad + mode_k
    column = place % TILE
    coef = coef_ref[...].astype(jnp.float32)
    height = plan.groups * plan.mode_pad
    total = jnp.zeros((height, TILE), jnp.float32)
    step = 1024 if count % 1024 == 0 else count
    row_iota = lax.broadcasted_iota(jnp.int32, (height, step), 0)
    column_iota = lax.broadcasted_iota(jnp.int32, (TILE, step), 0)
    for start in range(0, count, step):
        part = slice(start, start + step)
        left = jnp.where(row_iota == row[:, part], coef[:, part], 0.0).astype(jnp.bfloat16)
        right = jnp.where(column_iota == column[:, part], 1.0, 0.0).astype(jnp.bfloat16)
        total = total + lax.dot_general(
            left, right, (((1,), (1,)), ((), ())), preferred_element_type=jnp.float32
        )
    for g in range(plan.groups):
        table_ref[:, g * TILE : (g + 1) * TILE] = total[g * plan.mode_pad : (g + 1) * plan.mode_pad].astype(jnp.bfloat16)

    shape = (plan.wide_pad, plan.wide)
    column = lax.broadcasted_iota(jnp.int32, shape, 1)
    mode = lax.broadcasted_iota(jnp.int32, shape, 0)
    inner = column % plan.packed
    slot = jnp.where(
        inner < plan.fields, (column // plan.packed) * plan.slot_dev + inner // COMPS, -1
    )
    wanted = jnp.full(shape, -2, jnp.int32)
    for m in range(plan.modes):
        wanted = jnp.where(mode == m, slot_ref[m], wanted)
    hit = jnp.where(wanted == slot, 1.0, 0.0)
    pickers = [jnp.where(inner % COMPS == d, hit, 0.0) for d in range(COMPS)]
    pick_ref[...] = jnp.concatenate(pickers, axis=0).astype(jnp.bfloat16)
    narrow = jnp.concatenate([picker[: plan.mode_pad] for picker in pickers], axis=0)
    place_ref[...] = narrow.T.astype(jnp.bfloat16)
    swap_ref[...] = block_transposer(plan)


def contract_kernel(plan, got_ref, stencil_ref, table_ref, pick_ref, place_ref, out_ref, *scratch):
    conv_ref, beside_ref = scratch[:2]
    prod_refs, field_refs = scratch[2:4], (scratch[4:7], scratch[7:10])
    planes, inner, pad, main, wide = plan.planes, plan.inner, plan.mode_pad, plan.main, plan.wide_pad
    tail = plan.pairs + plan.rest_rows
    if tail < plan.depth:
        for ref in prod_refs:
            ref[tail:, :] = jnp.zeros((plan.depth - tail, ref.shape[1]), jnp.bfloat16)

    def vector(p, v):
        return got_ref[p % planes, :, v].reshape(plan.wide, LANES)

    centers = [jnp.concatenate([vector(p, v) for v in range(plan.vectors)], axis=1) for p in range(planes)]

    def slope_beside(first, last):
        row = jnp.concatenate(centers[first:last], axis=0)
        slopes = jnp.dot(row, stencil_ref[...], preferred_element_type=jnp.float32)
        beside_ref[first * plan.wide : last * plan.wide, :] = slopes.astype(jnp.bfloat16)

    def prepare(fields, p):
        moving_ref, row_ref, slope_ref = fields
        parts = [vector(p, v) for v in range(inner)]
        for v in range(inner):
            ahead, behind = vector(p + 1, v), vector(p - 1, v)
            parts.append((0.5 * (ahead.astype(jnp.float32) - behind.astype(jnp.float32))).astype(jnp.bfloat16))
        parts.append(beside_ref[p * plan.wide : (p + 1) * plan.wide, :])
        picked = jnp.dot(pick_ref[...], jnp.concatenate(parts, axis=1), preferred_element_type=jnp.float32)
        moving_ref[...] = picked[:, : inner * LANES]
        slopes = picked[:, inner * LANES :]
        slope_ref[...] = slopes.astype(jnp.bfloat16)
        for c in range(COMPS):
            row_ref[c * 8 : (c + 1) * 8] = slopes[c * wide + main : c * wide + main + 8]

    def repeated(row):
        return jnp.broadcast_to(row, (PACK, LANES)).astype(jnp.bfloat16)

    def along(left, right):
        term = left[0] * right[0]
        for d in range(1, COMPS):
            term = term + left[d] * right[d]
        return term

    def fill(prod_ref, fields, v):
        moving_ref, row_ref, slope_ref = fields
        here = slice(v * LANES, (v + 1) * LANES)

        def there(d):
            return slice((d * inner + v) * LANES, (d * inner + v + 1) * LANES)

        def lanes(c):
            return slice((v * COMPS + c) * LANES, (v * COMPS + c + 1) * LANES)

        slopes = {
            (c, j): [slope_ref[c * wide + j : c * wide + j + PACK, there(d)] for d in range(COMPS)]
            for c in range(COMPS)
            for j in range(0, main, PACK)
        }
        for i in range(plan.modes):
            moving = [repeated(moving_ref[d * wide + i : d * wide + i + 1, here]) for d in range(COMPS)]
            for c in range(COMPS):
                for j in range(0, main, PACK):
                    prod_ref[i * main + j : i * main + j + PACK, lanes(c)] = along(moving, slopes[c, j])
        if plan.rest:
            moving = {
                i: [moving_ref[d * wide + i : d * wide + i + PACK, here].astype(jnp.bfloat16) for d in range(COMPS)]
                for i in range(0, wide, PACK)
            }
            for c in range(COMPS):
                for j in range(plan.rest):
                    slope = [repeated(row_ref[c * 8 + j : c * 8 + j + 1, there(d)]) for d in range(COMPS)]
                    for i in range(0, wide, PACK):
                        at = plan.pairs + j * wide + i
                        prod_ref[at : at + PACK, lanes(c)] = along(moving[i], slope)

    def multiply(slot, prod_ref, cut):
        low, high = cut
        result = jnp.dot(table_ref[...], prod_ref[:, low:high], preferred_element_type=jnp.float32)
        for at in range(low, high, LANES):
            v, c = divmod(at // LANES, COMPS)
            conv_ref[slot, v, c * pad : (c + 1) * pad, :] = result[:, at - low : at - low + LANES]

    slope_beside(0, 1)
    prepare(field_refs[0], 0)
    slope_beside(1, planes)
    ready = []
    for p in range(planes):
        if p + 1 < planes:
            prepare(field_refs[(p + 1) % 2], p + 1)
        for v in range(inner):
            while ready:
                multiply(*ready.pop(0))
            fill(prod_refs[p % 2], field_refs[p % 2], v)
            done, filled = v * COMPS * LANES, (v + 1) * COMPS * LANES
            ready = [(p, prod_refs[p % 2], cut) for cut in plan.cuts if done < cut[1] <= filled]
    while ready:
        multiply(*ready.pop(0))
    for p in range(planes):
        stacked = jnp.concatenate([conv_ref[p, v].astype(jnp.bfloat16) for v in range(inner)], axis=1)
        placed = jnp.dot(place_ref[...], stacked, preferred_element_type=jnp.float32).astype(jnp.bfloat16)
        for v in range(inner):
            block = placed[:, v * LANES : (v + 1) * LANES]
            out_ref[p, :, v] = block.reshape(plan.chunks, plan.packed, LANES)


def finish_kernel(plan, got_ref, base_ref, swap_ref, conv_ref, next_ref, flat_ref, conv_vmem, next_vmem, sems):
    rows = [
        jnp.concatenate([got_ref[s, :, v].reshape(plan.wide, LANES) for s in range(plan.planes)], axis=1)
        for v in range(plan.inner)
    ]
    swapped = jnp.dot(jnp.concatenate(rows, axis=0), swap_ref[...], preferred_element_type=jnp.float32)
    for v in range(plan.inner):
        for block in range(min(plan.planes, plan.rows - v * plan.planes)):
            for chunk in range(plan.chunks):
                at = (chunk * plan.rows + v * plan.planes + block) * plan.packed
                first = v * plan.wide + chunk * plan.packed
                flat_ref[at : at + plan.packed, :] = swapped[
                    first : first + plan.packed, block * LANES : (block + 1) * LANES
                ]
    copies = []
    for s in range(plan.slot_dev):
        fields = slice(s * COMPS, (s + 1) * COMPS)
        for f in range(s * COMPS, (s + 1) * COMPS):
            value = flat_ref[pl.ds(f, plan.ny, stride=plan.packed), :]
            conv_vmem[f] = value
            next_vmem[f] = base_ref[f] - SECTION_STEP * value
        for which, (source, target) in enumerate(((conv_vmem, conv_ref), (next_vmem, next_ref))):
            copies.append(pltpu.make_async_copy(source.at[fields], target.at[fields], sems.at[which, s]))
            copies[-1].start()
    for copy in copies:
        copy.wait()


def on_device(velocity, base_velocity, mode_slot, triples, triple_coef):
    slot_dev, _, _, ny, nz = velocity.shape
    chunks, planes = lax.axis_size("chaos"), lax.axis_size("space")
    plan = Plan(slot_dev, ny, nz, planes, chunks, mode_slot.shape[0])
    fields, packed, devices = plan.fields, plan.packed, planes * chunks

    def exchange(block):
        flat = block.reshape((devices,) + block.shape[2:])
        return lax.all_to_all(flat, ("space", "chaos"), 0, 0, tiled=True).reshape(block.shape)

    sent = pl.pallas_call(
        functools.partial(pack_kernel, plan),
        out_shape=jax.ShapeDtypeStruct((planes, chunks, plan.vectors, packed, LANES), jnp.bfloat16),
        in_specs=[pl.BlockSpec(memory_space=pltpu.HBM)],
        out_specs=pl.BlockSpec(memory_space=pltpu.HBM),
        scratch_shapes=[
            pltpu.VMEM((fields * ny, nz), jnp.float32),
            pltpu.VMEM((planes, chunks, plan.vectors, packed, LANES), jnp.bfloat16),
            pltpu.SemaphoreType.DMA,
            pltpu.SemaphoreType.DMA((plan.vectors,)),
        ],
        compiler_params=params(PACK_VMEM_LIMIT),
        name="pack",
    )(velocity.reshape(fields * ny, nz))
    got = exchange(sent)
    table, pick, place, swap = pl.pallas_call(
        functools.partial(prepare_kernel, plan),
        out_shape=[
            jax.ShapeDtypeStruct((plan.mode_pad, plan.depth), jnp.bfloat16),
            jax.ShapeDtypeStruct((COMPS * plan.wide_pad, plan.wide), jnp.bfloat16),
            jax.ShapeDtypeStruct((plan.wide, COMPS * plan.mode_pad), jnp.bfloat16),
            jax.ShapeDtypeStruct((planes * LANES, planes * LANES), jnp.bfloat16),
        ],
        in_specs=[pl.BlockSpec(memory_space=pltpu.SMEM)] + [vmem_spec()] * 2,
        out_specs=[vmem_spec()] * 4,
        compiler_params=params(),
        name="prepare",
    )(mode_slot, triples.T, triple_coef.reshape(1, -1))
    returned = pl.pallas_call(
        functools.partial(contract_kernel, plan),
        out_shape=jax.ShapeDtypeStruct((planes, chunks, plan.inner, packed, LANES), jnp.bfloat16),
        in_specs=[vmem_spec()] * 5,
        out_specs=vmem_spec(),
        scratch_shapes=[
            pltpu.VMEM((planes, plan.inner, COMPS * plan.mode_pad, LANES), jnp.float32),
            pltpu.VMEM((planes * plan.wide, 2 * plan.inner * LANES), jnp.bfloat16),
            pltpu.VMEM((plan.depth, plan.lanes), jnp.bfloat16),
            pltpu.VMEM((plan.depth, plan.lanes), jnp.bfloat16),
        ]
        + [
            pltpu.VMEM((COMPS * plan.wide_pad, plan.inner * LANES), jnp.float32),
            pltpu.VMEM((COMPS * 8, plan.lanes), jnp.float32),
            pltpu.VMEM((COMPS * plan.wide_pad, plan.lanes), jnp.bfloat16),
        ]
        * 2,
        compiler_params=params(),
        name="contract",
    )(got, jnp.asarray(plan.stencil(), jnp.bfloat16), table, pick, place)
    convection, next_velocity = pl.pallas_call(
        functools.partial(finish_kernel, plan),
        out_shape=[jax.ShapeDtypeStruct((fields, ny, nz), jnp.float32)] * 2,
        in_specs=[vmem_spec()] * 3,
        out_specs=[pl.BlockSpec(memory_space=pl.ANY)] * 2,
        scratch_shapes=[
            pltpu.VMEM((ny * packed, LANES), jnp.float32),
            pltpu.VMEM((fields, ny, nz), jnp.float32),
            pltpu.VMEM((fields, ny, nz), jnp.float32),
            pltpu.SemaphoreType.DMA((2, slot_dev)),
        ],
        compiler_params=params(),
        name="finish",
    )(exchange(returned), base_velocity.reshape(fields, ny, nz), swap)
    return convection.reshape(velocity.shape), next_velocity.reshape(velocity.shape)


def solution(mesh):
    spread = P("chaos", None, "space", None, None)
    return jax.shard_map(
        on_device,
        mesh=mesh,
        in_specs=(spread, spread, P(), P(), P()),
        out_specs=(spread, spread),
        check_vma=False,
    )
```
